32 devices in a mesh: dp: 16 (over z, y, core), tensor: 2 (over x).
Axes of the slice: x: 2, y: 2, z: 4, core: 2. Of those that a mesh axis runs over, the one named last changes fastest.
Arguments:
- tokens: bfloat16 [21760, 1024], P(('dp', 'tensor')), may hold values from -6 to 6
- condition: bfloat16 [32, 1024], P('dp'), may hold values from -6 to 6
- scale_lens: int32 [32, 10], P('dp'), may hold values from 1 to 256, 680 in all within a row
- qkv_weight: bfloat16 [1024, 3, 1024], P('dp', None, 'tensor'), may hold values from -0.1875 to 0.1875
- qv_bias: bfloat16 [2, 1024], P(None, 'tensor'), may hold values from -3 to 3
- head_scale: float32 [16], P('tensor'), may hold values from 8 to 24
- proj_weight: bfloat16 [1024, 1024], P('tensor', 'dp'), may hold values from -0.75 to 0.75
- proj_bias: bfloat16 [1024], P('dp'), may hold values from -3 to 3
- fc1_weight: bfloat16 [1024, 4096], P('dp', 'tensor'), may hold values from -0.1875 to 0.1875
- fc1_bias: bfloat16 [4096], P('tensor'), may hold values from -3 to 3
- fc2_weight: bfloat16 [4096, 1024], P('tensor', 'dp'), may hold values from -0.09375 to 0.09375
- fc2_bias: bfloat16 [1024], P('dp'), may hold values from -3 to 3
- ada_weight: bfloat16 [1024, 6, 1024], P('dp', None, 'tensor'), may hold values from -0.1875 to 0.1875
- ada_bias: bfloat16 [6, 1024], P(None, 'tensor'), may hold values from -2 to 2
- cotangent: bfloat16 [21760, 1024], P(('dp', 'tensor')), may hold values from -6 to 6
Outputs:
- mixed: bfloat16 [21760, 1024], P(('dp', 'tensor'))
- grad_tokens: bfloat16 [21760, 1024], P(('dp', 'tensor'))
- grad_condition: float32 [32, 1024], P(('dp', 'tensor'))
- grad_qkv_weight: float32 [1024, 3, 1024], P('dp', None, 'tensor')
- grad_qv_bias: float32 [2, 1024], P(None, 'tensor')
- grad_head_scale: float32 [16], P('tensor')
- grad_proj_weight: float32 [1024, 1024], P('tensor', 'dp')
- grad_proj_bias: float32 [1024], P('dp')
- grad_fc1_weight: float32 [1024, 4096], P('dp', 'tensor')
- grad_fc1_bias: float32 [4096], P('tensor')
- grad_fc2_weight: float32 [4096, 1024], P('tensor', 'dp')
- grad_fc2_bias: float32 [1024], P('dp')
- grad_ada_weight: float32 [1024, 6, 1024], P('dp', None, 'tensor')
- grad_ada_bias: float32 [6, 1024], P(None, 'tensor')
The draws below stay inside these ranges and needn't reach their ends.
Inputs may be any that keep to these rules, and one draw needn't show every extreme that they name: `scale_lens`: the 10 lengths of each image sum to 680.
All inputs are finite; a program needn't handle non-finite values.
Results may differ from the reference program's by a relative error of at most 0.019.
Values may be sent and summed in bfloat16 or wider, within the bound.
No kernel may reach another device: no remote copies, remote signals or barrier semaphores. Data moves between devices by JAX's collectives and lax.ppermute only.
A program may use at most 256 MiB of HBM per device.

```python
import math
import jax
import jax.numpy as jnp
import numpy as np
from jax import lax

D = 1024
HEADS = 16
HEAD_DIM = 64
FF = 4096
COND = 1024
SCALES = 10
SEQ = 680
MOST = 256
IMG_GRP = 2
IMAGES = 32
TOKENS = 21760


def spiked(entries, rng, source, target, parts, factor):
    def block_of(dim):
        return (jnp.arange(entries.shape[dim]) // (entries.shape[dim] // parts)).reshape((-1,) + (1,) * (entries.ndim - 1 - dim))

    near = jax.random.permutation(rng, parts)[block_of(target)]
    far = (block_of(target) + parts // 2) % parts
    return jnp.where((block_of(source) == near) | (block_of(source) == far), factor * entries, entries)


def block_scale(rng, dims, cuts, low, top_value):
    def one(axis_at, shards_of):
        draws = jax.random.uniform(jax.random.fold_in(jax.random.fold_in(rng, 6), axis_at), (shards_of,), jnp.float32, low / len(cuts), top_value / len(cuts))
        return jnp.repeat(jnp.exp(draws), dims[axis_at] // shards_of).reshape((-1,) + (1,) * (len(dims) - axis_at - 1))

    factor_of = one(*cuts[0])
    for cut in cuts[1:]:
        factor_of = factor_of * one(*cut)
    return factor_of


def profile(number_of, total, limit, lean):
    portions = [(1 << 20) // math.isqrt(standing ** lean) + 1 for standing in range(2, number_of + 1)]
    surplus, holding = total - limit - (number_of - 1), [1] * (number_of - 1)
    while surplus > 0:
        movable = [i for i in range(number_of - 1) if holding[i] < limit]
        whole, remaining = sum([portions[i] for i in movable]), surplus
        for i in movable:
            extra = min(limit - holding[i], max(1, remaining * portions[i] // whole), surplus)
            holding[i] = holding[i] + extra
            surplus = surplus - extra
    return np.array([limit] + holding)


def ragged_sizes(own_key, number_of, total, bound, skew):
    if number_of == 2:
        one = jax.random.randint(own_key, (), max(1, total - bound), min(bound, total - 1) + 1)
        return jnp.stack([one, total - one])
    sizes = jnp.asarray(profile(number_of, total, bound, skew), jnp.int32)
    twos = (number_of - 1) // 2
    giver, sink = sizes[1:1 + 2 * twos:2], sizes[2:2 + 2 * twos:2]
    room = jnp.minimum(giver - 1, bound - sink)
    shifted = jax.random.randint(jax.random.fold_in(own_key, 1), (twos,), 0, 1 << 20) % (room + 1)
    sizes = sizes.at[1:1 + 2 * twos:2].set(giver - shifted).at[2:2 + 2 * twos:2].set(sink + shifted)
    return sizes[jax.random.permutation(jax.random.fold_in(own_key, 2), number_of)]


def gaussian(stream_key, extent, scale, reach, pieces=(), kind=jnp.bfloat16):
    array = jax.random.normal(stream_key, extent, jnp.float32) * scale
    if len(pieces) > 0:
        array = block_scale(stream_key, extent, pieces, -0.22, 0.18) * array
    return jnp.clip(array, min=-reach, max=reach).astype(kind)


def heavy_noise(rng, dims, deviation, bound, shards, heavy, kind=jnp.bfloat16):
    entries = deviation * jax.random.normal(rng, dims, jnp.float32)
    if shards:
        entries = entries * block_scale(rng, dims, shards, -0.22, 0.18)
    return jnp.clip(spiked(entries, jax.random.fold_in(rng, 3), *heavy), -bound, bound).astype(kind)


def setup_inputs(seed: int = 0) -> dict:
    splits = jax.random.split(jax.random.key(seed), 16)
    return {
        "tokens": gaussian(splits[0], (TOKENS, D), 1.0, 6.0, ((0, 32),)),
        "condition": gaussian(splits[1], (IMAGES, COND), 1.0, 6.0, ((0, 16),)),
        "scale_lens": jax.vmap(lambda own: ragged_sizes(own, SCALES, SEQ, MOST, 0))(jax.random.split(splits[2], IMAGES)).reshape((IMAGES, SCALES)).astype(jnp.int32),
        "qkv_weight": gaussian(splits[3], (D, 3, D), D ** -0.5, 0.1875, ((0, 16), (2, 2))),
        "qv_bias": gaussian(splits[4], (2, D), 0.5, 3.0, ((1, 2),)),
        "head_scale": jnp.clip(jnp.exp(math.log(24.0) - 1.0986123 * jax.random.uniform(splits[5], (HEADS,), jnp.float32) ** block_scale(splits[5], (HEADS,), ((0, 2),), -0.2, 0.2)), 8.0, 24.0),
        "proj_weight": gaussian(splits[6], (D, D), (D // 16) ** -0.5, 0.75, ((0, 2), (1, 16))),
        "proj_bias": gaussian(splits[7], (D,), 0.5, 3.0, ((0, 16),)),
        "fc1_weight": gaussian(splits[8], (D, FF), D ** -0.5, 0.1875, ((0, 16), (1, 2))),
        "fc1_bias": gaussian(splits[9], (FF,), 0.5, 3.0, ((0, 2),)),
        "fc2_weight": gaussian(splits[10], (FF, D), FF ** -0.5, 0.09375, ((0, 2), (1, 16))),
        "fc2_bias": gaussian(splits[11], (D,), 0.5, 3.0, ((0, 16),)),
        "ada_weight": gaussian(splits[12], (COND, 6, D), COND ** -0.5, 0.1875, ((0, 16), (2, 2))),
        "ada_bias": gaussian(splits[13], (6, D), 0.3, 2.0, ((1, 2),)),
        "cotangent": heavy_noise(splits[14], (TOKENS, D), 1.0, 6.0, ((0, 32),), (0, 1, 32, 2.75)),
    }


HIGHEST = lax.Precision.HIGHEST
NORM_EPS = 1e-06
HEAD_EPS = 1e-06
MASKED = -1e+30

@jax.custom_vjp
def low(v):
    return lax.optimization_barrier(v.astype(jnp.bfloat16)).astype(jnp.float32)

@jax.custom_vjp
def low_back(v):
    return v

def low_keep(v):
    return (low(v), None)

def low_pass(kept, grad):
    return (grad,)

def back_keep(v):
    return (v, None)

def back_low(kept, grad):
    return (low(grad),)
low.defvjp(low_keep, low_pass)
low_back.defvjp(back_keep, back_low)

def layer_norm(row_data):
    average = lax.optimization_barrier(jnp.mean(row_data, axis=-1, keepdims=True))
    centred = row_data - average
    variance = lax.optimization_barrier(jnp.mean(centred * centred, axis=-1, keepdims=True))
    return centred * lax.rsqrt(variance + NORM_EPS)

def modulate(row_data, scale_row, shift_row):
    return layer_norm(row_data) * (1.0 + scale_row) + shift_row

def unit_norm(values):
    return values * lax.rsqrt(lax.optimization_barrier(jnp.sum(values * values, axis=-1, keepdims=True)) + HEAD_EPS)

def scale_ids(lengths):
    bounds = jnp.cumsum(lengths).astype(jnp.int32)
    places = jnp.arange(SEQ, dtype=jnp.int32)
    return lax.optimization_barrier(jnp.sum((places[:, None] >= bounds[None, :]).astype(jnp.int32), axis=1))

def attend(operands):
    queries, key_rows, value_rows, lengths = operands
    scale_of = scale_ids(lengths)
    allowed = scale_of[None, :] <= scale_of[:, None]
    scores = jnp.einsum('qhd,khd->hqk', queries, key_rows, precision=HIGHEST)
    scores = low_back(jnp.where(allowed[None], scores, MASKED))
    row_max = lax.optimization_barrier(jnp.max(scores, axis=-1, keepdims=True))
    expo_terms = jnp.exp(scores - row_max)
    probability = low(expo_terms / lax.optimization_barrier(jnp.sum(expo_terms, axis=-1, keepdims=True)))
    return jnp.einsum('hqk,khd->qhd', probability, value_rows, precision=HIGHEST)

def block_forward(weights, row_data, cond_data, lengths):
    qkv_weight, qv_bias, head_scale, proj_weight, proj_bias, fc1_weight, fc1_bias, fc2_weight, fc2_bias, ada_weight, ada_bias = weights
    image_count = row_data.shape[0]
    cond_low = low(jax.nn.silu(cond_data))
    modulation = low_back(jnp.einsum('ic,csd->isd', cond_low, ada_weight, precision=HIGHEST) + ada_bias)
    mixed_one = low(modulate(row_data, modulation[:, 2:3], modulation[:, 4:5]))
    bias_rows = jnp.stack([qv_bias[0], jnp.zeros_like(qv_bias[0]), qv_bias[1]])
    qkv_rows = low_back(jnp.einsum('ntd,dsk->ntsk', mixed_one, qkv_weight, precision=HIGHEST) + bias_rows)
    shaped = (image_count, SEQ, HEADS, HEAD_DIM)
    queries = low(unit_norm(qkv_rows[:, :, 0].reshape(shaped)) * head_scale[:, None])
    key_rows = low(unit_norm(qkv_rows[:, :, 1].reshape(shaped)))
    value_rows = low(qkv_rows[:, :, 2].reshape(shaped))
    attended = lax.map(jax.checkpoint(attend), (queries, key_rows, value_rows, lengths))
    heads_low = low_back(low(attended.reshape(image_count, SEQ, D)))
    branch_one = low_back(jnp.einsum('ntk,kd->ntd', heads_low, proj_weight, precision=HIGHEST) + proj_bias)
    middle = row_data + modulation[:, 0:1] * branch_one
    mixed_two = low(modulate(middle, modulation[:, 3:4], modulation[:, 5:6]))
    hidden_pre = low_back(jnp.einsum('ntd,df->ntf', mixed_two, fc1_weight, precision=HIGHEST) + fc1_bias)
    hidden_low = low(jax.nn.gelu(hidden_pre, approximate=True))
    branch_two = low_back(jnp.einsum('ntf,fd->ntd', hidden_low, fc2_weight, precision=HIGHEST) + fc2_bias)
    return middle + modulation[:, 1:2] * branch_two

def reference(tokens, condition, scale_lens, qkv_weight, qv_bias, head_scale, proj_weight, proj_bias, fc1_weight, fc1_bias, fc2_weight, fc2_bias, ada_weight, ada_bias, cotangent):
    weights = tuple((weight_arg.astype(jnp.float32) for weight_arg in (qkv_weight, qv_bias, head_scale, proj_weight, proj_bias, fc1_weight, fc1_bias, fc2_weight, fc2_bias, ada_weight, ada_bias)))
    group_count = IMAGES // IMG_GRP
    token_groups = tokens.astype(jnp.float32).reshape(group_count, IMG_GRP, SEQ, D)
    cond_groups = condition.astype(jnp.float32).reshape(group_count, IMG_GRP, COND)
    length_groups = scale_lens.reshape(group_count, IMG_GRP, SCALES)
    grad_groups = cotangent.astype(jnp.float32).reshape(group_count, IMG_GRP, SEQ, D)

    def one_group(totals, group_batch):
        row_data, cond_data, lengths, grad_data = group_batch

        def forward(params, rows_in, cond_in):
            return block_forward(params, rows_in, cond_in, lengths)
        result, pullback = jax.vjp(forward, weights, row_data, cond_data)
        grad_weights, grad_rows, grad_cond = pullback(grad_data)
        totals = jax.tree.map(jnp.add, totals, grad_weights)
        return (totals, (result.astype(jnp.bfloat16), grad_rows.astype(jnp.bfloat16), grad_cond))
    initial = tuple((jnp.zeros_like(weight_arg) for weight_arg in weights))
    totals, (outputs, grad_rows, grad_cond) = lax.scan(one_group, initial, (token_groups, cond_groups, length_groups, grad_groups))
    return (outputs.reshape(TOKENS, D), grad_rows.reshape(TOKENS, D), grad_cond.reshape(IMAGES, COND), totals[0], totals[1], totals[2], totals[3], totals[4], totals[5], totals[6], totals[7], totals[8], totals[9], totals[10])
```

```python
import functools

import jax
import jax.numpy as jnp
from jax import lax
from jax.experimental import pallas as pl
from jax.experimental.pallas import tpu as pltpu
from jax.sharding import PartitionSpec as P

SEQ = 680
NORM_EPS = 1e-06
HEAD_EPS = 1e-06
MASKED = -1e30
HEAD = 64
LANES = 128
GELU_C = 0.7978845608
GELU_A = 0.044715
AXES = ("dp", "tensor")
BACK_AXES = ("tensor", "dp")
VMEM_BYTES = 56 * 1024 * 1024

F32 = jnp.float32
BF16 = jnp.bfloat16
VMEM = pl.BlockSpec(memory_space=pltpu.VMEM)
SMEM = pl.BlockSpec(memory_space=pltpu.SMEM)
ANY = pl.BlockSpec(memory_space=pl.ANY)


def dot(left, right):
    return lax.dot_general(left, right, (((1,), (0,)), ((), ())), preferred_element_type=F32)


def dot_nt(left, right):
    return lax.dot_general(left, right, (((1,), (1,)), ((), ())), preferred_element_type=F32)


def row_chunks(rows, size):
    return [(first, min(size, rows - first)) for first in range(0, rows, size)]


def call(kernel, out_shape, in_specs, out_specs, scratch, cost, name, grid=None, after=()):
    extra = {} if grid is None else {"grid": grid}
    count = len(in_specs)

    def body(*refs):
        kernel(*refs[:count], *refs[count + len(after) :])

    run = pl.pallas_call(
        body,
        out_shape=out_shape,
        in_specs=list(in_specs) + [ANY] * len(after),
        out_specs=out_specs,
        scratch_shapes=scratch,
        cost_estimate=pl.CostEstimate(
            flops=int(cost * 1e9), bytes_accessed=1 << 20, transcendentals=0
        ),
        compiler_params=pltpu.CompilerParams(vmem_limit_bytes=VMEM_BYTES),
        name=name,
        **extra,
    )
    return lambda *operands: run(*operands, *after)


def shape(*dims, dtype=F32):
    return jax.ShapeDtypeStruct(dims, dtype)


class Cube:
    def __init__(self, dp_size, tensor_size):
        self.dp_size, self.tensor_size = dp_size, tensor_size
        dp_bits = dp_size.bit_length() - 1
        tensor_bits = tensor_size.bit_length() - 1
        far = [("dp", 1 << bit) for bit in range(2, dp_bits)]
        near = [("dp", 2)]
        side = [("tensor", 1 << bit) for bit in reversed(range(tensor_bits))]
        core = [("dp", 1)]
        self.orders = (core + side + near + far, core + near + side + far)
        self.sum_orders = (side + near + far, near + side + far)
        self.near_hops = len(side) + 1
        self.core = core[0]
        self.devices = dp_size * tensor_size

    def hop(self, values, hop):
        axis, mask = hop
        size = self.dp_size if axis == "dp" else self.tensor_size
        return lax.ppermute(values, axis, [(i, i ^ mask) for i in range(size)])

    def masks(self, order, index):
        dp_mask, tensor_mask = 0, 0
        for place, (axis, mask) in enumerate(order):
            if (index >> (len(order) - 1 - place)) & 1:
                if axis == "dp":
                    dp_mask |= mask
                else:
                    tensor_mask |= mask
        return dp_mask, tensor_mask

    def index(self, order, dp_rel, tensor_rel):
        total = 0
        for place, (axis, mask) in enumerate(order):
            rel = dp_rel if axis == "dp" else tensor_rel
            bit = (rel // mask) % 2
            total = total + bit * (1 << (len(order) - 1 - place))
        return total

    @property
    def hops(self):
        return len(self.orders[0])


def behind(values, others):
    kept, unused = lax.optimization_barrier((values, others))
    return kept


class Gather:
    def __init__(self, cube, shard):
        self.cube = cube
        rows = shard.shape[0] // 2
        self.step = 0
        self.held = [shard[None, :rows], shard[None, rows:]]
        self.launch()

    def launch(self):
        hops = [order[len(order) - 1 - self.step] for order in self.cube.orders]
        self.received = [self.cube.hop(held, hop) for held, hop in zip(self.held, hops)]

    def advance(self, others=None):
        if others is not None:
            self.received = behind(self.received, others)
        self.step += 1
        self.held = [jnp.concatenate(pair, axis=0) for pair in zip(self.held, self.received)]
        self.launch()

    def sides(self):
        while self.step < self.cube.hops - 1:
            self.advance()
        return [self.held[0], self.received[0], self.held[1], self.received[1]]


class Scatter:
    def __init__(self, cube, groups):
        self.cube, self.step = cube, 0
        self.kept, self.received = [], []
        for group in groups:
            self.add(group)

    def add(self, pairs):
        self.kept.append([keep for keep, send in pairs])
        self.received.append(self.launch([send for keep, send in pairs]))

    def launch(self, outgoing):
        return [
            self.cube.hop(values, order[self.step])
            for values, order in zip(outgoing, self.cube.sum_orders)
        ]

    def advance(self, others=None):
        if self.step == self.cube.hops - 2:
            return []
        if others is not None:
            self.received = behind(self.received, others)
        self.step += 1
        merge = self.step >= self.cube.near_hops
        outs = add_pieces(self.kept, self.received, merge)
        self.kept = [list(outs[0::2])]
        if merge:
            self.received = [[self.cube.hop(outs[1], self.cube.sum_orders[0][self.step])]]
        else:
            self.received = [self.launch(outs[1::2])]
        return list(outs)

    def finish(self, others=None):
        while self.step < self.cube.hops - 2:
            self.advance()
        received = self.received if others is None else behind(self.received, others)
        return self.kept[0][0][0].astype(F32) + received[0][0][0].astype(F32)


def start_pieces(cube, place, held, columns, target, sem):
    copies = make_pieces(cube, place, held, columns, target, sem)
    for copy in copies:
        copy.start()
    return copies


def make_pieces(cube, place, held, columns, target, sem):
    dp_at, tensor_at = place[0], place[1]
    first, count = columns
    half = cube.devices // 2
    copies = []
    for part, order in enumerate(cube.orders):
        for side in range(2):
            source = held[2 * part + side]
            rows = source.shape[1]
            for item in range(half):
                dp_mask, tensor_mask = cube.masks(order, side * half + item)
                owner = jnp.bitwise_xor(dp_at, dp_mask)
                tensor_owner = jnp.bitwise_xor(tensor_at, tensor_mask)
                row = pl.multiple_of(owner * (2 * rows) + part * rows, 16)
                copies.append(
                    pltpu.make_async_copy(
                        source.at[item, :, pl.ds(first, count)],
                        target.at[tensor_owner, pl.ds(row, rows), :],
                        sem,
                    )
                )
    return copies


def moments(values):
    average = jnp.mean(values, axis=-1, keepdims=True)
    centred = values - average
    variance = jnp.mean(centred * centred, axis=-1, keepdims=True)
    return centred, lax.rsqrt(variance + NORM_EPS)


def head_ones():
    row = lax.broadcasted_iota(jnp.int32, (LANES, LANES), 0) // HEAD
    col = lax.broadcasted_iota(jnp.int32, (LANES, LANES), 1) // HEAD
    return (row == col).astype(BF16)


def head_sums(values, ones):
    high = values.astype(BF16)
    low = (values - high.astype(F32)).astype(BF16)
    return dot(high, ones) + dot(low, ones)


def front_kernel(
    cube, pieces, place, tokens, parts, h0, h1, h2, h3,
    mixed, query, key, value, r_query, r_key, modul, fc1_bias, head_scale,
    weight, sem, qv_bias,
):
    copies = start_pieces(cube, place, (h0, h1, h2, h3), (0, weight.shape[2]), weight, sem)
    rows, width = tokens.shape
    local = width // cube.tensor_size
    wide = fc1_bias.shape[1] // cube.tensor_size
    share = (3 * local + wide) // pieces
    last = parts.shape[2] - share
    for item in range(cube.tensor_size):
        for kind in range(6):
            at = slice(kind * local, (kind + 1) * local)
            total = parts[0, item : item + 1, at]
            for source in range(1, cube.dp_size):
                total = total + parts[source, item : item + 1, at]
            modul[kind : kind + 1, item * local : (item + 1) * local] = total
        for piece in range(pieces):
            for step in range(0, share, LANES):
                at = piece * share + step
                got = parts[piece, item : item + 1, last + step : last + step + LANES]
                kind, inner = at // local, at % local
                if kind < 2:
                    qv_bias[kind : kind + 1, pl.ds(item * local + inner, LANES)] = got
                elif kind == 2:
                    head_scale[0:1, pl.ds(item * local + inner, LANES)] = got
                else:
                    fc1_bias[0:1, pl.ds(item * wide + at - 3 * local, LANES)] = got
    modul[6:8, :] = jnp.zeros((2, width), F32)
    gain = 1.0 + modul[2:3, :]
    shift = modul[4:5, :]
    for first, count in row_chunks(rows, 64):
        centred, scale = moments(tokens[first : first + count, :].astype(F32))
        mixed[first : first + count, :] = (centred * scale * gain + shift).astype(BF16)
    for copy in copies:
        copy.wait()
    ones = head_ones()
    for item in range(cube.tensor_size):
        for kind in range(3):
            out = dot(mixed[...], weight[item, :, kind * local : (kind + 1) * local])
            for slab in range(local // LANES):
                at = item * local + slab * LANES
                cols = slice(at, at + LANES)
                part = out[:, slab * LANES : (slab + 1) * LANES]
                if kind == 0:
                    part = part + qv_bias[0:1, cols]
                if kind == 2:
                    value[:, cols] = (part + qv_bias[1:2, cols]).astype(BF16)
                    continue
                inverse = lax.rsqrt(head_sums(part * part, ones) + HEAD_EPS)
                unit = part * inverse
                if kind == 0:
                    query[:, cols] = (unit * head_scale[0:1, cols]).astype(BF16)
                    r_query[:, cols] = inverse
                else:
                    key[:, cols] = unit.astype(BF16)
                    r_key[:, cols] = inverse


def lane_index(rows):
    return lax.broadcasted_iota(jnp.int32, (rows, LANES), 1)


def attend_kernel(query, key, value, query_code, key_code, heads, log_sum):
    rows = query.shape[0]
    low = lane_index(rows) < HEAD
    q, k, v = query[...], key[...], value[...]
    qc, kc = query_code[...], key_code[...]
    zero = jnp.zeros_like(v)
    keys = (jnp.where(low, k, kc), jnp.where(low, kc, k))
    queries = (jnp.where(low, q, qc), jnp.where(low, qc, q))
    values = (jnp.where(low, v, zero), jnp.where(low, zero, v))
    for first, count in row_chunks(rows, 352):
        at = slice(first, first + count)
        out, logs = jnp.zeros((count, LANES), F32), []
        for head in range(2):
            expo = jnp.exp(dot_nt(queries[head][at], keys[head]))
            total = jnp.sum(expo, axis=1, keepdims=True)
            out = out + dot((expo * (1.0 / total)).astype(BF16), values[head])
            logs.append(jnp.log(total))
        heads[at, :] = out.astype(BF16)
        log_sum[at, :] = jnp.where(lane_index(count) < HEAD, logs[1], logs[0])


def middle_kernel(
    cube, place, heads, tokens, cotangent, modul, proj_bias, h0, h1, h2, h3,
    branch, middle, mixed, gated_sum, weight, sem,
):
    rows, width = tokens.shape
    local = width // cube.tensor_size
    copies = start_pieces(cube, place, (h0, h1, h2, h3), (3 * local, local), weight, sem)
    for copy in copies:
        copy.wait()
    gain = 1.0 + modul[3:4, :]
    shift = modul[5:6, :]
    gamma = modul[0:1, :]
    gamma_two = modul[1:2, :]
    total = jnp.zeros((1, width), F32)
    for first, count in row_chunks(rows, 176):
        at = slice(first, first + count)
        out = proj_bias[0:1, :] + jnp.zeros((count, width), F32)
        for item in range(cube.tensor_size):
            out = out + dot_nt(
                heads[at, item * local : (item + 1) * local], weight[item]
            )
        branch[at, :] = out
        mid = tokens[at, :].astype(F32) + gamma * out
        middle[at, :] = mid
        centred, scale = moments(mid)
        mixed[0, at, :] = (centred * scale * gain + shift).astype(BF16)
        gated = (cotangent[at, :].astype(F32) * gamma_two).astype(BF16)
        mixed[1, at, :] = gated
        total += jnp.sum(gated.astype(F32), axis=0, keepdims=True)
    gated_sum[...] = total


def hidden_kernel(mixed, bias, matrix, hidden, slope):
    rows = mixed.shape[0]
    weight = matrix[...].reshape(mixed.shape[1], matrix.shape[2])
    for first, count in row_chunks(rows, 352):
        at = slice(first, first + count)
        pre = dot(mixed[at, :], weight) + bias[...]
        square = pre * pre
        bent = jnp.tanh(pre * (GELU_C + (GELU_C * GELU_A) * square))
        half = 0.5 * pre
        hidden[at, :] = (half + half * bent).astype(BF16)
        slope[at, :] = (
            0.5
            + 0.5 * bent
            + half * (1.0 - bent * bent) * (GELU_C + (3.0 * GELU_C * GELU_A) * square)
        )


def pre_back_kernel(slope, gated, matrix, grad_pre, bias_sums):
    weight = matrix[...].reshape(gated.shape[1], matrix.shape[2])
    low = (dot(gated[...], weight) * slope[...]).astype(BF16)
    grad_pre[...] = low
    bias_sums[...] = jnp.sum(low.astype(F32), axis=0, keepdims=True)


def add_products(total, left, matrix):
    weight = matrix[...].reshape(total.shape[1], matrix.shape[2])

    @pl.when(pl.program_id(0) == 0)
    def _():
        total[...] = dot_nt(left[...], weight)

    @pl.when(pl.program_id(0) > 0)
    def _():
        total[...] += dot_nt(left[...], weight)


def output_kernel(
    steps, hidden, matrix, cotangent, middle, modul, fc2_bias, output, sums,
    total, cotangent_here, middle_here, sem,
):
    step = pl.program_id(0)
    copies = [
        pltpu.make_async_copy(cotangent, cotangent_here, sem.at[0]),
        pltpu.make_async_copy(middle, middle_here, sem.at[1]),
    ]

    @pl.when(step == 0)
    def _():
        for copy in copies:
            copy.start()

    add_products(total, hidden, matrix)

    @pl.when(step == steps - 1)
    def _():
        for copy in copies:
            copy.wait()
        rows, width = total.shape
        gamma = modul[1:2, :]
        gamma_sum = jnp.zeros((1, width), F32)
        for first, count in row_chunks(rows, 64):
            at = slice(first, first + count)
            out = total[at, :] + fc2_bias[...]
            output[at, :] = (middle_here[at, :] + gamma * out).astype(BF16)
            gamma_sum += jnp.sum(
                cotangent_here[at, :].astype(F32) * out, axis=0, keepdims=True
            )
        sums[...] = gamma_sum


def first_back_kernel(
    cube, steps, place, grad_pre, matrix, middle, branch, cotangent, modul, h0, h1, h2, h3,
    g_middle, gated, g_heads, sums,
    total, middle_here, branch_here, cotangent_here, gated_here, small, sem, small_sem,
):
    step = pl.program_id(0)
    rows, width = total.shape
    narrow = small.shape[2]
    copies = [
        pltpu.make_async_copy(middle, middle_here, sem.at[0]),
        pltpu.make_async_copy(branch, branch_here, sem.at[1]),
        pltpu.make_async_copy(cotangent, cotangent_here, sem.at[2]),
    ]
    small_copies = make_pieces(
        cube, place, (h0, h1, h2, h3), (3 * narrow, narrow), small, small_sem
    )
    outs = [
        pltpu.make_async_copy(total, g_middle, sem.at[0]),
        pltpu.make_async_copy(gated_here, gated, sem.at[1]),
    ]

    @pl.when(step == 0)
    def _():
        for copy in copies + small_copies:
            copy.start()

    add_products(total, grad_pre, matrix)

    @pl.when(step == steps - 1)
    def _():
        for copy in copies:
            copy.wait()
        gain = 1.0 + modul[3:4, :]
        gamma = modul[0:1, :]
        totals = [jnp.zeros((1, width), F32) for _ in range(4)]
        for first, count in row_chunks(rows, 64):
            at = slice(first, first + count)
            grad = total[at, :]
            centred, scale = moments(middle_here[at, :])
            normed = centred * scale
            totals[0] += jnp.sum(grad * normed, axis=0, keepdims=True)
            totals[1] += jnp.sum(grad, axis=0, keepdims=True)
            lifted = grad * gain
            back = cotangent_here[at, :].astype(F32) + scale * (
                lifted
                - jnp.mean(lifted, axis=-1, keepdims=True)
                - normed * jnp.mean(lifted * normed, axis=-1, keepdims=True)
            )
            total[at, :] = back
            totals[2] += jnp.sum(back * branch_here[at, :], axis=0, keepdims=True)
            low = (back * gamma).astype(BF16)
            gated_here[at, :] = low
            totals[3] += jnp.sum(low.astype(F32), axis=0, keepdims=True)
        for place_at in range(4):
            sums[place_at : place_at + 1, :] = totals[place_at]
        for copy in outs:
            copy.start()
        for copy in small_copies:
            copy.wait()
        for item in range(cube.tensor_size):
            g_heads[:, item * narrow : (item + 1) * narrow] = dot(
                gated_here[...], small[item]
            ).astype(BF16)
        for copy in outs:
            copy.wait()


def core_rows(cube, place, target, source):
    rows, width = source.shape
    piece = width // cube.dp_size
    here = place[0] % 2 == 0
    for slab in range(width // LANES):
        flipped = source[:, slab * LANES : (slab + 1) * LANES].T
        for pair in range(LANES // (2 * piece)):
            at = 2 * pair * piece
            at_target = slab * LANES // 2 + pair * piece
            target[at_target : at_target + piece, :] = jnp.where(
                here, flipped[at : at + piece], flipped[at + piece : at + 2 * piece]
            )


def pieces_out(cube, place, item, table, outs, sem, first, count):
    dp_at, tensor_at = place[0], place[1]
    tensor_rel = jnp.bitwise_xor(tensor_at, item)
    piece = table.shape[1] * 2 // cube.dp_size
    for pair in range(cube.dp_size // 2):
        dp_rel = jnp.bitwise_xor(dp_at - dp_at % 2, 2 * pair)
        for part, order in enumerate(cube.sum_orders):
            keep, send = outs[2 * part], outs[2 * part + 1]
            half, rows = keep.shape[0], keep.shape[1]
            index = cube.index(order, dp_rel, tensor_rel)
            source = table.at[item, pl.ds(pair * piece + part * rows, rows), :]
            away = index >= half

            @pl.when(away)
            def _():
                pltpu.make_async_copy(
                    source, send.at[index - half, :, pl.ds(first, count)], sem
                ).start()

            @pl.when(jnp.logical_not(away))
            def _():
                pltpu.make_async_copy(
                    source, keep.at[index, :, pl.ds(first, count)], sem
                ).start()


def wait_pieces(cube, item, table, outs, sem, first, count):
    for pair in range(cube.dp_size // 2):
        for part in range(2):
            keep = outs[2 * part]
            rows = keep.shape[1]
            pltpu.make_async_copy(
                table.at[item, pl.ds(0, rows), :], keep.at[0, :, pl.ds(first, count)], sem
            ).wait()


def wide_grad_kernel(cube, per, place, left, left_far, right, right_far, *refs):
    outs, (flip, table, sem) = refs[:-3], refs[-3:]
    step = pl.program_id(0)
    local, block = table.shape[2], right.shape[1]

    @pl.when(step == 0)
    def _():
        core_rows(cube, place, flip.at[0], left)
        core_rows(cube, place, flip.at[1], left_far)

    got = (dot(flip[0], right[...]) + dot(flip[1], right_far[...])).astype(BF16)
    for item in range(cube.tensor_size):
        for part in range(per):

            @pl.when(step == item * per + part)
            def _():
                table[item, :, part * block : (part + 1) * block] = got
                if part == per - 1:
                    pieces_out(cube, place, item, table, outs, sem, 0, local)

    @pl.when(step == cube.tensor_size * per - 1)
    def _():
        for item in range(cube.tensor_size):
            wait_pieces(cube, item, table, outs, sem, 0, local)


def qkv_grad_kernel(cube, with_proj, place, mixed, mixed_far, grads, grads_far, *refs):
    if with_proj:
        gated, gated_far, heads, heads_far = refs[:4]
        outs, refs = refs[4:8], refs[8:]
        flip, table, mat, mat_far, own, far, sem, in_sem, small, sides, sides_far = refs
    else:
        outs, refs = refs[:4], refs[4:]
        flip, table, mat, mat_far, own, far, sem, in_sem = refs
    copies = [
        pltpu.make_async_copy(source, target, in_sem.at[place_at])
        for place_at, (source, target) in enumerate(
            ((mixed, mat), (mixed_far, mat_far), (grads, own), (grads_far, far))
        )
    ]
    if with_proj:
        copies += [
            pltpu.make_async_copy(source, target, in_sem.at[4 + place_at])
            for place_at, (source, target) in enumerate(((heads, sides), (heads_far, sides_far)))
        ]
    for copy in copies:
        copy.start()
    local = table.shape[2] // 3
    for copy in copies[:2]:
        copy.wait()
    core_rows(cube, place, flip.at[0], mat)
    core_rows(cube, place, flip.at[1], mat_far)
    if with_proj:
        late = [
            pltpu.make_async_copy(source, target, in_sem.at[place_at])
            for place_at, (source, target) in enumerate(((gated, mat), (gated_far, mat_far)))
        ]
        for copy in late:
            copy.start()
    for copy in copies[2:4]:
        copy.wait()
    for item in range(cube.tensor_size):
        cols = slice(item * local, (item + 1) * local)
        for kind in range(3):
            table[item, :, kind * local : (kind + 1) * local] = (
                dot(flip[0], own[kind, :, cols]) + dot(flip[1], far[kind, :, cols])
            ).astype(BF16)
        pieces_out(cube, place, item, table, outs, sem, 0, 3 * local)
    if with_proj:
        narrow = small.shape[2]
        for copy in late + copies[4:]:
            copy.wait()
        core_rows(cube, place, flip.at[0], mat)
        core_rows(cube, place, flip.at[1], mat_far)
        for item in range(cube.tensor_size):
            cols = slice(item * narrow, (item + 1) * narrow)
            small[item] = (dot(flip[0], sides[:, cols]) + dot(flip[1], sides_far[:, cols])).astype(
                BF16
            )
            pieces_out(cube, place, item, small, outs, sem, 3 * local, narrow)
        for item in range(cube.tensor_size):
            wait_pieces(cube, item, small, outs, sem, 3 * local, narrow)
    for item in range(cube.tensor_size):
        wait_pieces(cube, item, table, outs, sem, 0, 3 * local)


def split_into(base, lanes, start, values):
    high = values.astype(BF16)
    rest = (values - high.astype(F32)).astype(BF16)
    base = jnp.where(lanes == start, high, base)
    return jnp.where(lanes == start + 1, rest, base)


def attend_back_kernel(
    query, key, value, grad, log_sum, r_query, r_key, head_scale, query_code, key_code,
    grads, sums, flat_query, sides, pairs,
):
    rows = query.shape[0]
    step = pairs.shape[1] // 2
    lanes = lane_index(rows)
    low = lanes < HEAD
    inner = lanes % HEAD
    q, k, v, g = query[...], key[...], value[...], grad[...]
    ones = head_ones()
    spare = 16
    zero = jnp.zeros((rows, LANES), BF16)
    one = jnp.ones((rows, LANES), BF16)
    marks = (inner == spare) | (inner == spare + 1)

    @pl.when(pl.program_id(0) == 0)
    def _():
        pairs[...] = jnp.zeros_like(pairs)
        sides[...] = jnp.zeros_like(sides)

    qc = split_into(query_code[...], inner, spare, -log_sum[...])
    high = jnp.logical_not(low)
    q_wide = jnp.concatenate([q, qc], axis=1)
    for head in range(2):
        side = low if head == 0 else high
        k_code = jnp.where(marks & (high if head == 0 else low), one, key_code[...])
        k_side = jnp.where(side, k, zero)
        k_wide = jnp.concatenate([k_side, k_code], axis=1)
        v_side = jnp.where(side, v, zero)
        at = slice(head * step, head * step + rows)
        sides[0, at, :] = jnp.where(side, g, zero)
        sides[1, at, :] = jnp.where(side, q, zero)
        probs = jnp.exp(dot_nt(k_wide, q_wide))
        pairs[0:rows, at] = probs.astype(BF16)
        weighted = probs * dot_nt(v_side, g)
        change = (weighted - probs * jnp.sum(weighted, axis=0, keepdims=True)).astype(BF16)
        pairs[step : step + rows, at] = change
        flat = dot(k_side.T, change)
        if head == 0:
            flat_query[...] = flat
        else:
            flat_query[...] += flat
    d_value = dot(pairs[0:rows, :], sides[0]).astype(BF16)
    d_key = dot(pairs[step : step + rows, :], sides[1])
    d_query = flat_query[...].T
    scale = head_scale[0:1, :]
    unit = q.astype(F32) / scale
    along = head_sums(unit * d_query, ones)
    out = (r_query[...] * scale * (d_query - unit * along)).astype(BF16)
    grads[0] = out
    sums[0:1, :] = jnp.sum(out.astype(F32), axis=0, keepdims=True)
    sums[2:3, :] = jnp.sum(along, axis=0, keepdims=True)
    unit_key = k.astype(F32)
    along_key = head_sums(unit_key * d_key, ones)
    grads[1] = (r_key[...] * (d_key - unit_key * along_key)).astype(BF16)
    grads[2] = d_value
    sums[1:2, :] = jnp.sum(d_value.astype(F32), axis=0, keepdims=True)


def last_kernel(cube, splits, place, modul, tokens, g_middle, h0, h1, h2, h3, *refs):
    grads, refs = refs[: len(splits)], refs[len(splits) :]
    grad_tokens, sums, weight, left, tokens_here, middle_here, sem, in_sem = refs[:8]
    grads_here = refs[8:]
    rows, width = tokens_here.shape
    local = width // cube.tensor_size
    copies = [
        pltpu.make_async_copy(source, target, in_sem.at[place_at])
        for place_at, (source, target) in enumerate(
            list(zip(grads, grads_here)) + [(tokens, tokens_here), (g_middle, middle_here)]
        )
    ]
    for copy in copies:
        copy.start()
    pieces = make_pieces(cube, place, (h0, h1, h2, h3), (0, weight.shape[2]), weight, sem)
    for copy in pieces:
        copy.start()
    for which, (start, size) in enumerate(splits):
        copies[which].wait()
        for item in range(cube.tensor_size):
            for kind in range(3):
                at = kind * local + start
                left[item, :, at : at + size] = grads_here[which][
                    kind, :, item * size : (item + 1) * size
                ]
    for copy in copies[len(splits) :] + pieces:
        copy.wait()
    gain = 1.0 + modul[2:3, :]
    totals = [jnp.zeros((1, width), F32) for _ in range(2)]
    for first, count in row_chunks(rows, 352):
        out = dot_nt(left[0, first : first + count, :], weight[0])
        for item in range(1, cube.tensor_size):
            out = out + dot_nt(left[item, first : first + count, :], weight[item])
        for inner, inner_count in row_chunks(count, 64):
            at = slice(first + inner, first + inner + inner_count)
            grad = out[inner : inner + inner_count]
            centred, scale = moments(tokens_here[at, :].astype(F32))
            normed = centred * scale
            totals[0] += jnp.sum(grad * normed, axis=0, keepdims=True)
            totals[1] += jnp.sum(grad, axis=0, keepdims=True)
            lifted = grad * gain
            back = middle_here[at, :] + scale * (
                lifted
                - jnp.mean(lifted, axis=-1, keepdims=True)
                - normed * jnp.mean(lifted * normed, axis=-1, keepdims=True)
            )
            grad_tokens[at, :] = back.astype(BF16)
    for place_at in range(2):
        sums[place_at : place_at + 1, :] = totals[place_at]


def pack_kernel(splits, sums_one, gamma_sum, sums_zero, fc1_bias_sum, gated_sum, *refs):
    parts, (out, side) = refs[: len(splits)], refs[len(splits) :]
    dp_size = side.shape[0]
    tensor_size = out.shape[0] // dp_size
    width = gamma_sum.shape[1]
    local, wide = width // tensor_size, fc1_bias_sum.shape[1] // tensor_size
    owners = LANES * dp_size // width
    for slab in range(width // LANES):
        cols = slice(slab * LANES, (slab + 1) * LANES)
        rows = slice(slab * owners, (slab + 1) * owners)
        side[rows, 0:LANES] = jnp.broadcast_to(gated_sum[:, cols], (owners, LANES))
        side[rows, LANES : 2 * LANES] = jnp.broadcast_to(sums_one[3:4, cols], (owners, LANES))
    modul = (
        sums_one[2:3, :], gamma_sum[...], sums_zero[0:1, :],
        sums_one[0:1, :], sums_zero[1:2, :], sums_one[1:2, :],
    )
    for item in range(tensor_size):
        rows = slice(item * dp_size, (item + 1) * dp_size)

        def put(at, values):
            count = values.shape[1]
            out[rows, at : at + count] = jnp.broadcast_to(values, (dp_size, count)).astype(BF16)

        for kind, values in enumerate(modul):
            put(kind * local, values[:, item * local : (item + 1) * local])
        for kind in range(3):
            for part, (start, size) in zip(parts, splits):
                at = (6 + kind) * local + start
                values = part[kind : kind + 1, item * size : (item + 1) * size]
                put(at, values)
                if kind == 2:
                    put(at + local, values - values.astype(BF16).astype(F32))
        put(10 * local, fc1_bias_sum[:, item * wide : (item + 1) * wide])
        out[rows, 10 * local + wide :] = side[...].astype(BF16)


def add_kernel(parts, groups, merge, *refs):
    outs = refs[4 * parts * groups :]
    at = 0
    for part in range(parts):
        first = 0
        for group in range(groups):
            for side in range(2):
                kept, received = refs[at], refs[at + 1]
                at += 2
                rows, count = kept.shape[1:]
                total = (kept[...].astype(F32) + received[...].astype(F32)).astype(BF16)
                base = part * rows if merge else 0
                out = outs[side] if merge else outs[2 * part + side]
                out[:, base : base + rows, first : first + count] = total
            first += count


def add_pieces(kept, received, merge):
    groups, parts = len(kept), len(kept[0])
    items, rows = kept[0][0].shape[0], kept[0][0].shape[1]
    half = items // 2
    per = max(1, half // 2)
    columns = sum(group[0].shape[2] for group in kept)
    operands, specs = [], []
    for part in range(parts):
        for group in range(groups):
            block = (per, rows, kept[group][part].shape[2])
            for side in range(2):
                spec = pl.BlockSpec(block, lambda i, side=side: (i + side * (half // per), 0, 0))
                operands += [kept[group][part], received[group][part]]
                specs += [spec, spec]
    out_rows, out_parts = (parts * rows, 1) if merge else (rows, parts)
    return pl.pallas_call(
        functools.partial(add_kernel, parts, groups, merge),
        out_shape=[jax.ShapeDtypeStruct((half, out_rows, columns), BF16)] * (2 * out_parts),
        grid=(half // per,),
        in_specs=specs,
        out_specs=[pl.BlockSpec((per, out_rows, columns), lambda i: (i, 0, 0))] * (2 * out_parts),
        cost_estimate=pl.CostEstimate(flops=1 << 20, bytes_accessed=1 << 20, transcendentals=0),
        compiler_params=pltpu.CompilerParams(vmem_limit_bytes=VMEM_BYTES),
        name="add",
    )(*operands)


def scale_codes(lengths, rows):
    count = lengths.shape[0]
    bounds = jnp.cumsum(lengths)
    places = jnp.arange(rows, dtype=jnp.int32)
    scale_of = jnp.sum((places[:, None] >= bounds[None, :]).astype(jnp.int32), axis=1)
    lane = jnp.arange(HEAD, dtype=jnp.int32)
    query_code = (scale_of[:, None] == lane[None, :]).astype(BF16)
    blocked = (scale_of[:, None] > lane[None, :]) & (lane[None, :] < count)
    key_code = jnp.where(blocked, MASKED, 0.0).astype(BF16)
    return jnp.tile(query_code, (1, 2)), jnp.tile(key_code, (1, 2))


def to_all(values, axes=AXES):
    return lax.all_to_all(values, axes, split_axis=0, concat_axis=0, tiled=True)


def local(
    tokens, condition, scale_lens, qkv_weight, qv_bias, head_scale, proj_weight, proj_bias,
    fc1_weight, fc1_bias, fc2_weight, fc2_bias, ada_weight, ada_bias, cotangent,
):
    dp_size, tensor_size = lax.axis_size("dp"), lax.axis_size("tensor")
    devices = dp_size * tensor_size
    cube = Cube(dp_size, tensor_size)
    dp_at, tensor_at = lax.axis_index("dp"), lax.axis_index("tensor")
    place = jnp.stack([dp_at, tensor_at]).astype(jnp.int32)
    rows, width = tokens.shape
    piece_rows = qkv_weight.shape[0]
    narrow = qkv_weight.shape[2]
    wide = fc1_weight.shape[1]
    hidden_width = wide * tensor_size

    cond_float = condition.astype(F32)
    cond_low = jax.nn.silu(cond_float).astype(BF16)
    cond_parts = cond_low.reshape(tensor_size, dp_size, piece_rows).transpose(1, 0, 2)
    cond_own = lax.all_to_all(cond_parts, "dp", split_axis=0, concat_axis=0, tiled=True)
    cond_back = cond_own.reshape(dp_size, tensor_size, piece_rows).transpose(1, 0, 2)
    cond_back = cond_back.reshape(devices, piece_rows)
    cond_own = cond_own.reshape(devices, piece_rows)
    ada_flat = ada_weight.reshape(piece_rows, 6 * narrow)

    narrow_gather = Gather(
        cube,
        jnp.concatenate([qkv_weight.reshape(piece_rows, 3 * narrow), proj_weight.T], axis=1),
    )
    narrow_gather.advance(cond_own)
    while narrow_gather.step < cube.hops - 4:
        narrow_gather.advance()
    wide_shard = jnp.concatenate([fc1_weight, fc2_weight.T], axis=1)
    wide_all = lax.all_gather(
        behind(wide_shard, narrow_gather.held), AXES, axis=0, tiled=True
    ).reshape(dp_size, tensor_size, piece_rows, 2 * wide)
    while narrow_gather.step < cube.hops - 2:
        narrow_gather.advance()

    modul_part = jnp.dot(cond_own, ada_flat, preferred_element_type=F32)
    bias_part = jnp.where(dp_at == 0, ada_bias.astype(F32).reshape(1, 6 * narrow), 0.0)
    dp_part = jnp.concatenate([proj_bias, fc2_bias]).astype(F32)
    tensor_part = jnp.concatenate(
        [qv_bias.astype(F32).reshape(-1), jnp.repeat(head_scale, HEAD), fc1_bias.astype(F32)]
    )
    share = -(-tensor_part.shape[0] // (dp_size * LANES)) * LANES
    pieces = tensor_part.shape[0] // share
    tensor_share = lax.dynamic_index_in_dim(
        tensor_part.reshape(pieces, share), jnp.minimum(dp_at, pieces - 1), 0, keepdims=False
    )
    rest = jnp.concatenate([dp_part, tensor_share])[None]
    parts = to_all(
        jnp.concatenate(
            [modul_part + bias_part, jnp.broadcast_to(rest, (devices, rest.shape[1]))], axis=1
        )
    ).reshape(dp_size, tensor_size, -1)
    narrow_gather.advance(parts)
    held = narrow_gather.sides()
    rest = parts[:, 0, 6 * narrow :]
    proj_bias_full = rest[:, :piece_rows].reshape(1, width)
    fc2_bias_full = rest[:, piece_rows : 2 * piece_rows].reshape(1, width)

    own_lens = lax.dynamic_index_in_dim(scale_lens, tensor_at, 0, keepdims=False)
    query_code, key_code = scale_codes(own_lens, rows)

    dma = pltpu.SemaphoreType.DMA

    def half_shape(*dims):
        return shape(*dims, dtype=BF16)

    mixed_one, query, key, value, r_query, r_key, modul, fc1_bias_full, head_scale_full = call(
        functools.partial(front_kernel, cube, pieces),
        [half_shape(rows, width)] * 4
        + [shape(rows, width)] * 2
        + [shape(8, width), shape(1, hidden_width), shape(1, width)],
        [SMEM, VMEM, VMEM] + [ANY] * 4,
        [VMEM] * 9,
        [
            pltpu.VMEM((tensor_size, width, 3 * narrow), BF16),
            dma,
            pltpu.VMEM((2, width), F32),
        ],
        16, "front",
    )(place, tokens, parts, *held)
    mixed_one_far = cube.hop(mixed_one, cube.core)

    slab = pl.BlockSpec((rows, LANES), lambda i: (0, i))
    whole = pl.BlockSpec((rows, LANES), lambda i: (0, 0))
    heads, log_sum = call(
        attend_kernel,
        [half_shape(rows, width), shape(rows, width)],
        [slab] * 3 + [whole] * 2,
        [slab] * 2,
        [],
        20, "attend", grid=(width // LANES,),
    )(query, key, value, query_code, key_code)
    heads_far = cube.hop(heads, cube.core)

    branch, middle, mixed_two, gated_sum = call(
        functools.partial(middle_kernel, cube),
        [shape(rows, width)] * 2 + [half_shape(2, rows, width), shape(1, width)],
        [SMEM] + [VMEM] * 5 + [ANY] * 4,
        [VMEM] * 4,
        [pltpu.VMEM((tensor_size, width, narrow), BF16), dma],
        10, "middle", after=[mixed_one_far],
    )(place, heads, tokens, cotangent, modul, proj_bias_full, *held)
    mixed_two_far = cube.hop(mixed_two, cube.core)

    block = min(1024, wide)
    per = wide // block
    wide_steps = tensor_size * per

    def wide_block(first):
        return pl.BlockSpec(
            (dp_size, None, piece_rows, block), lambda i: (0, i // per, 0, first * per + i % per)
        )

    side = pl.BlockSpec((rows, block), lambda i: (0, i))
    side_row = pl.BlockSpec((1, block), lambda i: (0, i))

    def mixed_part(which):
        return pl.BlockSpec((None, rows, width), lambda i: (which, 0, 0))

    hidden, slope = call(
        hidden_kernel,
        [half_shape(rows, hidden_width), shape(rows, hidden_width)],
        [mixed_part(0), side_row, wide_block(0)],
        [side] * 2,
        [],
        20, "hidden", grid=(wide_steps,), after=[heads_far],
    )(mixed_two, fc1_bias_full, wide_all)
    hidden_far = cube.hop(hidden, cube.core)

    grad_pre, fc1_bias_sum = call(
        pre_back_kernel,
        [half_shape(rows, hidden_width), shape(1, hidden_width)],
        [side, mixed_part(1), wide_block(1)],
        [side, side_row],
        [],
        300, "pre_back", grid=(wide_steps,), after=[mixed_two_far],
    )(slope, mixed_two, wide_all)
    grad_pre_far = cube.hop(grad_pre, cube.core)

    def piece_shapes(columns):
        return [half_shape(devices // 4, piece_rows // 2, columns)] * 4

    def pairs(outs):
        return list(zip(outs[0::2], outs[1::2]))

    flip_scratch = pltpu.VMEM((2, width // 2, rows), BF16)
    grad_scratch = [flip_scratch, pltpu.VMEM((tensor_size, width // 2, wide), BF16), dma]

    def wide_grad(which, right, right_far, name, after):
        return call(
            functools.partial(wide_grad_kernel, cube, per),
            piece_shapes(wide),
            [SMEM] + [mixed_part(which)] * 2 + [side] * 2,
            [ANY] * 4,
            grad_scratch,
            300, name, grid=(wide_steps,), after=after,
        )(place, mixed_two, mixed_two_far, right, right_far)

    outs = wide_grad(1, hidden, hidden_far, "fc2_grad", [grad_pre])
    fc2_sum = Scatter(cube, [pairs(outs)])
    outs = wide_grad(0, grad_pre, grad_pre_far, "fc1_grad", [outs[0]])
    fc1_sum = Scatter(cube, [pairs(outs)])

    full = pltpu.VMEM((rows, width), F32)
    full_half = pltpu.VMEM((rows, width), BF16)
    whole_row = pl.BlockSpec((1, width), lambda i: (0, 0))
    eight_rows = pl.BlockSpec((8, width), lambda i: (0, 0))
    whole_half = pl.BlockSpec((rows, width), lambda i: (0, 0))
    g_middle, gated_one, g_heads, sums_one = call(
        functools.partial(first_back_kernel, cube, wide_steps),
        [
            shape(rows, width),
            half_shape(rows, width),
            half_shape(rows, width),
            shape(8, width),
        ],
        [SMEM, side, wide_block(0)] + [ANY] * 3 + [eight_rows] + [ANY] * 4,
        [ANY, ANY, whole_half, eight_rows],
        [
            full, full, full, full_half, full_half,
            pltpu.VMEM((tensor_size, width, narrow), BF16),
            dma((3,)), dma,
        ],
        500, "first_back", grid=(wide_steps,), after=[outs[0]],
    )(place, grad_pre, wide_all, middle, branch, cotangent, modul, *held)
    gated_one_far = cube.hop(gated_one, cube.core)

    splits = [(0, narrow // 2), (narrow // 2, narrow // 2)]
    if narrow < 2 * LANES:
        splits = [(0, narrow)]
    steps = narrow // LANES
    padded = -(-rows // LANES) * LANES

    def attend_back(start, size, after):
        per, base = size // LANES, start // LANES

        def column(i):
            return (i // per) * steps + base + i % per

        picked = pl.BlockSpec((rows, LANES), lambda i: (0, column(i)))
        picked_row = pl.BlockSpec((1, LANES), lambda i: (0, column(i)))
        count = tensor_size * per
        return call(
            attend_back_kernel,
            [half_shape(3, rows, count * LANES), shape(8, count * LANES)],
            [picked] * 7 + [picked_row] + [whole] * 2,
            [
                pl.BlockSpec((3, rows, LANES), lambda i: (0, 0, i)),
                pl.BlockSpec((8, LANES), lambda i: (0, i)),
            ],
            [
                pltpu.VMEM((LANES, rows), F32),
                pltpu.VMEM((2, 2 * padded, LANES), BF16),
                pltpu.VMEM((2 * padded, 2 * padded), BF16),
            ],
            400, "attend_back", grid=(count,), after=after,
        )(query, key, value, g_heads, log_sum, r_query, r_key, head_scale_full,
          query_code, key_code)

    def qkv_grad(size, with_proj, grads, grads_far, after):
        extra = [gated_one, gated_one_far, heads, heads_far] if with_proj else []
        cut = pltpu.VMEM((3, rows, tensor_size * size), BF16)
        proj_scratch = [pltpu.VMEM((tensor_size, width // 2, narrow), BF16), full_half, full_half]
        return call(
            functools.partial(qkv_grad_kernel, cube, with_proj),
            piece_shapes(3 * size + (narrow if with_proj else 0)),
            [SMEM] + [ANY] * (4 + len(extra)),
            [ANY] * 4,
            [
                flip_scratch,
                pltpu.VMEM((tensor_size, width // 2, 3 * size), BF16),
                full_half, full_half, cut, cut,
                dma, dma((6,)),
            ] + (proj_scratch if with_proj else []),
            200, "qkv_grad", after=after,
        )(place, mixed_one, mixed_one_far, grads, grads_far, *extra)

    after = fc2_sum.advance(sums_one)
    qkv_grads, qkv_grads_far, all_sums = [], [], []
    for start, size in splits:
        grads, part_sums = attend_back(start, size, after)
        qkv_grads.append(grads)
        all_sums.append(part_sums)
        qkv_grads_far.append(cube.hop(grads, cube.core))
        after = [grads] + fc2_sum.advance(part_sums) + fc1_sum.advance(part_sums)
        if len(all_sums) == 1:
            after += [gated_one_far]
    qkv_sum = Scatter(cube, [])
    for which, (start, size) in enumerate(splits):
        outs = qkv_grad(size, which == 0, qkv_grads[which], qkv_grads_far[which], after)
        qkv_sum.add(pairs(outs))
        after = [outs[0]]
    fc2_received = fc2_sum.received
    after += fc1_sum.advance(outs[0])
    output, gamma_sum = call(
        functools.partial(output_kernel, wide_steps),
        [half_shape(rows, width), shape(1, width)],
        [side, wide_block(1)] + [ANY] * 2 + [eight_rows, whole_row],
        [whole_half, whole_row],
        [full, full_half, full, dma((2,))],
        400, "output", grid=(wide_steps,), after=after + [fc2_received[0][0]],
    )(hidden, wide_all, cotangent, middle, modul, fc2_bias_full)
    fc1_received = fc1_sum.received
    after = qkv_sum.advance(gamma_sum) + [fc1_received[0][0]]
    grad_tokens, sums_zero = call(
        functools.partial(last_kernel, cube, splits),
        [half_shape(rows, width), shape(8, width)],
        [SMEM, VMEM] + [ANY] * (6 + len(splits)),
        [VMEM] * 2,
        [
            pltpu.VMEM((tensor_size, width, 3 * narrow), BF16),
            pltpu.VMEM((tensor_size, rows, 3 * narrow), BF16),
            full_half, full, dma, dma((2 + len(splits),)),
        ]
        + [pltpu.VMEM((3, rows, tensor_size * size), BF16) for start, size in splits],
        400, "last", after=after,
    )(place, modul, tokens, g_middle, *held, *qkv_grads)

    landed = qkv_sum.received
    qkv_sum.advance(sums_zero)
    fc2_own = fc2_sum.finish(sums_zero)
    fc1_own = fc1_sum.finish(sums_zero)

    late = call(
        functools.partial(pack_kernel, splits),
        half_shape(devices, 10 * narrow + wide + 2 * LANES),
        [VMEM] * (5 + len(splits)),
        VMEM,
        [pltpu.VMEM((dp_size, 2 * LANES), F32)],
        1, "pack",
    )(sums_one, gamma_sum, sums_zero, fc1_bias_sum, gated_sum, *all_sums)
    late = to_all(behind(late, landed), BACK_AXES)
    grad_modul_all = late[:, : 6 * narrow]
    late_sum = jnp.sum(late.astype(F32), axis=0)
    grad_ada_bias = late_sum[: 6 * narrow].reshape(6, narrow)
    grad_qv_bias = late_sum[6 * narrow : 8 * narrow].reshape(2, narrow)
    head_sum = late_sum[8 * narrow : 9 * narrow] + late_sum[9 * narrow : 10 * narrow]
    grad_head_scale = head_sum.reshape(-1, HEAD)[:, 0]
    rest = late_sum[10 * narrow :]
    grad_fc1_bias = rest[:wide]
    first_own = (dp_at % (LANES // piece_rows)) * piece_rows
    own_rows = lax.dynamic_slice_in_dim(rest[wide:].reshape(2, LANES), first_own, piece_rows, axis=1)
    grad_fc2_bias, grad_proj_bias = own_rows[0], own_rows[1]
    grad_ada = lax.dot_general(
        cond_back, grad_modul_all, (((0,), (0,)), ((), ())), preferred_element_type=F32
    ).reshape(piece_rows, 6, narrow)
    cond_part = dot_nt(grad_modul_all, ada_flat)
    qkv_sum.advance(cond_part)
    own = qkv_sum.finish()
    parts_own, first = [], 0
    for which, (start, size) in enumerate(splits):
        parts_own.append(own[:, first : first + 3 * size].reshape(piece_rows, 3, size))
        first += 3 * size
        if which == 0:
            proj_own = own[:, first : first + narrow].T
            first += narrow
    qkv_own = jnp.concatenate(parts_own, axis=2)

    cond_all = to_all(cond_part, BACK_AXES).reshape(tensor_size, dp_size, piece_rows)
    cond_image = lax.dynamic_slice_in_dim(cond_float, tensor_at, 1, axis=0)
    unused, silu_back = jax.vjp(jax.nn.silu, cond_image)
    grad_condition = silu_back(jnp.sum(cond_all, axis=0).reshape(1, width))[0]

    return (
        output,
        grad_tokens,
        grad_condition,
        qkv_own,
        grad_qv_bias,
        grad_head_scale,
        proj_own,
        grad_proj_bias,
        fc1_own,
        grad_fc1_bias,
        fc2_own.T,
        grad_fc2_bias,
        grad_ada,
        grad_ada_bias,
    )


def solution(mesh):
    return jax.shard_map(
        local,
        mesh=mesh,
        in_specs=(
            P(("dp", "tensor"), None),
            P("dp", None),
            P("dp", None),
            P("dp", None, "tensor"),
            P(None, "tensor"),
            P("tensor"),
            P("tensor", "dp"),
            P("dp"),
            P("dp", "tensor"),
            P("tensor"),
            P("tensor", "dp"),
            P("dp"),
            P("dp", None, "tensor"),
            P(None, "tensor"),
            P(("dp", "tensor"), None),
        ),
        out_specs=(
            P(("dp", "tensor"), None),
            P(("dp", "tensor"), None),
            P(("dp", "tensor"), None),
            P("dp", None, "tensor"),
            P(None, "tensor"),
            P("tensor"),
            P("tensor", "dp"),
            P("dp"),
            P("dp", "tensor"),
            P("tensor"),
            P("tensor", "dp"),
            P("dp"),
            P("dp", None, "tensor"),
            P(None, "tensor"),
        ),
        check_vma=False,
    )
```

```python
import functools

import jax
import jax.numpy as jnp
from jax import lax
from jax.experimental import pallas as pl
from jax.experimental.pallas import tpu as pltpu
from jax.sharding import PartitionSpec as P

SEQ = 680
NORM_EPS = 1e-06
HEAD_EPS = 1e-06
MASKED = -1e30
HEAD = 64
LANES = 128
GELU_C = 0.7978845608
GELU_A = 0.044715
AXES = ("dp", "tensor")
BACK_AXES = ("tensor", "dp")
VMEM_BYTES = 56 * 1024 * 1024

F32 = jnp.float32
BF16 = jnp.bfloat16
VMEM = pl.BlockSpec(memory_space=pltpu.VMEM)
SMEM = pl.BlockSpec(memory_space=pltpu.SMEM)
ANY = pl.BlockSpec(memory_space=pl.ANY)


def dot(left, right):
    return lax.dot_general(left, right, (((1,), (0,)), ((), ())), preferred_element_type=F32)


def dot_nt(left, right):
    return lax.dot_general(left, right, (((1,), (1,)), ((), ())), preferred_element_type=F32)


def row_chunks(rows, size):
    return [(first, min(size, rows - first)) for first in range(0, rows, size)]


def call(
    kernel, out_shape, in_specs, out_specs, scratch, cost, name, grid=None, after=(), scalars=0
):
    count = len(in_specs) + scalars
    in_specs = list(in_specs) + [ANY] * len(after)
    if scalars:
        extra = {
            "grid_spec": pltpu.PrefetchScalarGridSpec(
                num_scalar_prefetch=scalars,
                grid=grid,
                in_specs=in_specs,
                out_specs=out_specs,
                scratch_shapes=scratch,
            )
        }
    else:
        extra = {"in_specs": in_specs, "out_specs": out_specs, "scratch_shapes": scratch}
        if grid is not None:
            extra["grid"] = grid

    def body(*refs):
        kernel(*refs[:count], *refs[count + len(after) :])

    run = pl.pallas_call(
        body,
        out_shape=out_shape,
        cost_estimate=pl.CostEstimate(
            flops=int(cost * 1e9), bytes_accessed=1 << 20, transcendentals=0
        ),
        compiler_params=pltpu.CompilerParams(vmem_limit_bytes=VMEM_BYTES),
        name=name,
        **extra,
    )
    return lambda *operands: run(*operands, *after)


def shape(*dims, dtype=F32):
    return jax.ShapeDtypeStruct(dims, dtype)


class Cube:
    def __init__(self, dp_size, tensor_size):
        self.dp_size, self.tensor_size = dp_size, tensor_size
        dp_bits = dp_size.bit_length() - 1
        tensor_bits = tensor_size.bit_length() - 1
        far = [("dp", 1 << bit) for bit in range(2, dp_bits)]
        near = [("dp", 2)]
        side = [("tensor", 1 << bit) for bit in reversed(range(tensor_bits))]
        core = [("dp", 1)]
        self.orders = (core + side + near + far, core + near + side + far)
        self.sum_orders = (side + near + far, near + side + far)
        self.near_hops = len(side) + 1
        self.core = core[0]
        self.devices = dp_size * tensor_size

    def hop(self, values, hop):
        axis, mask = hop
        size = self.dp_size if axis == "dp" else self.tensor_size
        return lax.ppermute(values, axis, [(i, i ^ mask) for i in range(size)])

    def masks(self, order, index):
        dp_mask, tensor_mask = 0, 0
        for place, (axis, mask) in enumerate(order):
            if (index >> (len(order) - 1 - place)) & 1:
                if axis == "dp":
                    dp_mask |= mask
                else:
                    tensor_mask |= mask
        return dp_mask, tensor_mask

    def index(self, order, dp_rel, tensor_rel):
        total = 0
        for place, (axis, mask) in enumerate(order):
            rel = dp_rel if axis == "dp" else tensor_rel
            bit = (rel // mask) % 2
            total = total + bit * (1 << (len(order) - 1 - place))
        return total

    @property
    def hops(self):
        return len(self.orders[0])


def behind(values, others):
    kept, unused = lax.optimization_barrier((values, others))
    return kept


class Gather:
    def __init__(self, cube, shard):
        self.cube = cube
        rows = shard.shape[0] // 2
        self.step = 0
        self.held = [shard[None, :rows], shard[None, rows:]]
        self.launch()

    def launch(self):
        hops = [order[len(order) - 1 - self.step] for order in self.cube.orders]
        self.received = [self.cube.hop(held, hop) for held, hop in zip(self.held, hops)]

    def advance(self, others=None):
        if others is not None:
            self.received = behind(self.received, others)
        self.step += 1
        self.held = [jnp.concatenate(pair, axis=0) for pair in zip(self.held, self.received)]
        self.launch()

    def sides(self, others=None):
        crossed = [self.cube.hop(held, self.cube.core) for held in self.held]
        if others is not None:
            self.received = behind(self.received, others)
        got = []
        for held, received, other in zip(self.held, self.received, crossed):
            got += [held, received, other, self.cube.hop(received, self.cube.core)]
        return got


class Scatter:
    def __init__(self, cube, groups):
        self.cube, self.step = cube, 0
        self.kept, self.received = [], []
        for group in groups:
            self.add(group)

    def add(self, pairs):
        self.kept.append([keep for keep, send in pairs])
        self.received.append(self.launch([send for keep, send in pairs]))

    def launch(self, outgoing):
        return [
            self.cube.hop(values, order[self.step])
            for values, order in zip(outgoing, self.cube.sum_orders)
        ]

    def advance(self, others=None):
        if self.step == self.cube.hops - 2:
            return []
        if others is not None:
            self.received = behind(self.received, others)
        self.step += 1
        merge = self.step >= self.cube.near_hops
        outs = add_pieces(self.kept, self.received, merge)
        self.kept = [list(outs[0::2])]
        if merge:
            self.received = [[self.cube.hop(outs[1], self.cube.sum_orders[0][self.step])]]
        else:
            self.received = [self.launch(outs[1::2])]
        return list(outs)

    def finish(self, others=None):
        while self.step < self.cube.hops - 2:
            self.advance()
        received = self.received if others is None else behind(self.received, others)
        return self.kept[0][0][0].astype(F32) + received[0][0][0].astype(F32)


def start_pieces(cube, place, held, columns, target, sem):
    copies = make_pieces(cube, place, held, columns, target, sem)
    for copy in copies:
        copy.start()
    return copies


def make_pieces(cube, place, held, columns, target, sem):
    dp_at, tensor_at = place[0], place[1]
    first, count = columns
    quarter = cube.devices // 4
    copies = []
    for part, order in enumerate(cube.orders):
        for side in range(4):
            source = held[4 * part + side]
            rows = source.shape[1]
            for item in range(quarter):
                dp_mask, tensor_mask = cube.masks(order, side * quarter + item)
                owner = jnp.bitwise_xor(dp_at, dp_mask)
                tensor_owner = jnp.bitwise_xor(tensor_at, tensor_mask)
                row = pl.multiple_of(owner * (2 * rows) + part * rows, 16)
                copies.append(
                    pltpu.make_async_copy(
                        source.at[item, :, pl.ds(first, count)],
                        target.at[tensor_owner, pl.ds(row, rows), :],
                        sem,
                    )
                )
    return copies


def moments(values):
    average = jnp.mean(values, axis=-1, keepdims=True)
    centred = values - average
    variance = jnp.mean(centred * centred, axis=-1, keepdims=True)
    return centred, lax.rsqrt(variance + NORM_EPS)


def head_ones():
    row = lax.broadcasted_iota(jnp.int32, (LANES, LANES), 0) // HEAD
    col = lax.broadcasted_iota(jnp.int32, (LANES, LANES), 1) // HEAD
    return (row == col).astype(BF16)


def head_sums(values, ones):
    high = values.astype(BF16)
    low = (values - high.astype(F32)).astype(BF16)
    return dot(high, ones) + dot(low, ones)


def front_kernel(
    cube, pieces, place, tokens, parts, h0, h1, h2, h3, h4, h5, h6, h7,
    mixed, query, key, value, r_query, r_key, modul, fc1_bias, head_scale,
    weight, sem, qv_bias,
):
    copies = start_pieces(cube, place, (h0, h1, h2, h3, h4, h5, h6, h7), (0, weight.shape[2]), weight, sem)
    rows, width = tokens.shape
    local = width // cube.tensor_size
    wide = fc1_bias.shape[1] // cube.tensor_size
    share = (3 * local + wide) // pieces
    last = parts.shape[2] - share
    for item in range(cube.tensor_size):
        for kind in range(6):
            at = slice(kind * local, (kind + 1) * local)
            total = parts[0, item : item + 1, at]
            for source in range(1, cube.dp_size):
                total = total + parts[source, item : item + 1, at]
            modul[kind : kind + 1, item * local : (item + 1) * local] = total
        for piece in range(pieces):
            for step in range(0, share, LANES):
                at = piece * share + step
                got = parts[piece, item : item + 1, last + step : last + step + LANES]
                kind, inner = at // local, at % local
                if kind < 2:
                    qv_bias[kind : kind + 1, pl.ds(item * local + inner, LANES)] = got
                elif kind == 2:
                    head_scale[0:1, pl.ds(item * local + inner, LANES)] = got
                else:
                    fc1_bias[0:1, pl.ds(item * wide + at - 3 * local, LANES)] = got
    modul[6:8, :] = jnp.zeros((2, width), F32)
    gain = 1.0 + modul[2:3, :]
    shift = modul[4:5, :]
    for first, count in row_chunks(rows, 64):
        centred, scale = moments(tokens[first : first + count, :].astype(F32))
        mixed[first : first + count, :] = (centred * scale * gain + shift).astype(BF16)
    for copy in copies:
        copy.wait()
    ones = head_ones()
    for item in range(cube.tensor_size):
        for kind in range(3):
            out = dot(mixed[...], weight[item, :, kind * local : (kind + 1) * local])
            for slab in range(local // LANES):
                at = item * local + slab * LANES
                cols = slice(at, at + LANES)
                part = out[:, slab * LANES : (slab + 1) * LANES]
                if kind == 0:
                    part = part + qv_bias[0:1, cols]
                if kind == 2:
                    value[:, cols] = (part + qv_bias[1:2, cols]).astype(BF16)
                    continue
                inverse = lax.rsqrt(head_sums(part * part, ones) + HEAD_EPS)
                unit = part * inverse
                if kind == 0:
                    query[:, cols] = (unit * head_scale[0:1, cols]).astype(BF16)
                    r_query[:, cols] = inverse
                else:
                    key[:, cols] = unit.astype(BF16)
                    r_key[:, cols] = inverse


def lane_index(rows):
    return lax.broadcasted_iota(jnp.int32, (rows, LANES), 1)


def attend_kernel(query, key, value, query_code, key_code, heads, log_sum):
    rows = query.shape[0]
    low = lane_index(rows) < HEAD
    q, k, v = query[...], key[...], value[...]
    qc, kc = query_code[...], key_code[...]
    zero = jnp.zeros_like(v)
    keys = (jnp.where(low, k, kc), jnp.where(low, kc, k))
    queries = (jnp.where(low, q, qc), jnp.where(low, qc, q))
    values = (jnp.where(low, v, zero), jnp.where(low, zero, v))
    for first, count in row_chunks(rows, 352):
        at = slice(first, first + count)
        out, logs = jnp.zeros((count, LANES), F32), []
        for head in range(2):
            expo = jnp.exp(dot_nt(queries[head][at], keys[head]))
            total = jnp.sum(expo, axis=1, keepdims=True)
            out = out + dot((expo * (1.0 / total)).astype(BF16), values[head])
            logs.append(jnp.log(total))
        heads[at, :] = out.astype(BF16)
        log_sum[at, :] = jnp.where(lane_index(count) < HEAD, logs[1], logs[0])


def middle_kernel(
    cube, place, heads, tokens, cotangent, modul, proj_bias, h0, h1, h2, h3, h4, h5, h6, h7,
    branch, middle, mixed, gated_sum, weight, sem,
):
    rows, width = tokens.shape
    local = width // cube.tensor_size
    copies = start_pieces(cube, place, (h0, h1, h2, h3, h4, h5, h6, h7), (3 * local, local), weight, sem)
    for copy in copies:
        copy.wait()
    gain = 1.0 + modul[3:4, :]
    shift = modul[5:6, :]
    gamma = modul[0:1, :]
    gamma_two = modul[1:2, :]
    total = jnp.zeros((1, width), F32)
    for first, count in row_chunks(rows, 176):
        at = slice(first, first + count)
        out = proj_bias[0:1, :] + jnp.zeros((count, width), F32)
        for item in range(cube.tensor_size):
            out = out + dot_nt(
                heads[at, item * local : (item + 1) * local], weight[item]
            )
        branch[at, :] = out
        mid = tokens[at, :].astype(F32) + gamma * out
        middle[at, :] = mid
        centred, scale = moments(mid)
        mixed[0, at, :] = (centred * scale * gain + shift).astype(BF16)
        gated = (cotangent[at, :].astype(F32) * gamma_two).astype(BF16)
        mixed[1, at, :] = gated
        total += jnp.sum(gated.astype(F32), axis=0, keepdims=True)
    gated_sum[...] = total


def hidden_kernel(mixed, bias, matrix, hidden, slope):
    rows = mixed.shape[0]
    weight = matrix[...].reshape(mixed.shape[1], matrix.shape[2])
    for first, count in row_chunks(rows, 352):
        at = slice(first, first + count)
        pre = dot(mixed[at, :], weight) + bias[...]
        square = pre * pre
        bent = jnp.tanh(pre * (GELU_C + (GELU_C * GELU_A) * square))
        half = 0.5 * pre
        hidden[at, :] = (half + half * bent).astype(BF16)
        slope[at, :] = (
            0.5
            + 0.5 * bent
            + half * (1.0 - bent * bent) * (GELU_C + (3.0 * GELU_C * GELU_A) * square)
        )


def pre_back_kernel(slope, gated, matrix, grad_pre, bias_sums):
    weight = matrix[...].reshape(gated.shape[1], matrix.shape[2])
    low = (dot(gated[...], weight) * slope[...]).astype(BF16)
    grad_pre[...] = low
    bias_sums[...] = jnp.sum(low.astype(F32), axis=0, keepdims=True)


def add_products(total, left, matrix):
    weight = matrix[...].reshape(total.shape[1], matrix.shape[2])

    @pl.when(pl.program_id(0) == 0)
    def _():
        total[...] = dot_nt(left[...], weight)

    @pl.when(pl.program_id(0) > 0)
    def _():
        total[...] += dot_nt(left[...], weight)


def output_kernel(
    steps, hidden, matrix, cotangent, middle, modul, fc2_bias, output, sums,
    total, cotangent_here, middle_here, sem,
):
    step = pl.program_id(0)
    copies = [
        pltpu.make_async_copy(cotangent, cotangent_here, sem.at[0]),
        pltpu.make_async_copy(middle, middle_here, sem.at[1]),
    ]

    @pl.when(step == 0)
    def _():
        for copy in copies:
            copy.start()

    add_products(total, hidden, matrix)

    @pl.when(step == steps - 1)
    def _():
        for copy in copies:
            copy.wait()
        rows, width = total.shape
        gamma = modul[1:2, :]
        gamma_sum = jnp.zeros((1, width), F32)
        for first, count in row_chunks(rows, 64):
            at = slice(first, first + count)
            out = total[at, :] + fc2_bias[...]
            output[at, :] = (middle_here[at, :] + gamma * out).astype(BF16)
            gamma_sum += jnp.sum(
                cotangent_here[at, :].astype(F32) * out, axis=0, keepdims=True
            )
        sums[...] = gamma_sum


def first_back_kernel(
    cube, steps, place, grad_pre, matrix, middle, branch, cotangent, modul, h0, h1, h2, h3, h4, h5, h6, h7,
    g_middle, gated, g_heads, sums,
    total, middle_here, branch_here, cotangent_here, gated_here, small, sem, small_sem,
):
    step = pl.program_id(0)
    rows, width = total.shape
    narrow = small.shape[2]
    copies = [
        pltpu.make_async_copy(middle, middle_here, sem.at[0]),
        pltpu.make_async_copy(branch, branch_here, sem.at[1]),
        pltpu.make_async_copy(cotangent, cotangent_here, sem.at[2]),
    ]
    small_copies = make_pieces(
        cube, place, (h0, h1, h2, h3, h4, h5, h6, h7), (3 * narrow, narrow), small, small_sem
    )
    outs = [
        pltpu.make_async_copy(total, g_middle, sem.at[0]),
        pltpu.make_async_copy(gated_here, gated, sem.at[1]),
    ]

    @pl.when(step == 0)
    def _():
        for copy in copies + small_copies:
            copy.start()

    add_products(total, grad_pre, matrix)

    @pl.when(step == steps - 1)
    def _():
        for copy in copies:
            copy.wait()
        gain = 1.0 + modul[3:4, :]
        gamma = modul[0:1, :]
        totals = [jnp.zeros((1, width), F32) for _ in range(4)]
        for first, count in row_chunks(rows, 64):
            at = slice(first, first + count)
            grad = total[at, :]
            centred, scale = moments(middle_here[at, :])
            normed = centred * scale
            totals[0] += jnp.sum(grad * normed, axis=0, keepdims=True)
            totals[1] += jnp.sum(grad, axis=0, keepdims=True)
            lifted = grad * gain
            back = cotangent_here[at, :].astype(F32) + scale * (
                lifted
                - jnp.mean(lifted, axis=-1, keepdims=True)
                - normed * jnp.mean(lifted * normed, axis=-1, keepdims=True)
            )
            total[at, :] = back
            totals[2] += jnp.sum(back * branch_here[at, :], axis=0, keepdims=True)
            low = (back * gamma).astype(BF16)
            gated_here[at, :] = low
            totals[3] += jnp.sum(low.astype(F32), axis=0, keepdims=True)
        for place_at in range(4):
            sums[place_at : place_at + 1, :] = totals[place_at]
        for copy in outs:
            copy.start()
        for copy in small_copies:
            copy.wait()
        for item in range(cube.tensor_size):
            g_heads[:, item * narrow : (item + 1) * narrow] = dot(
                gated_here[...], small[item]
            ).astype(BF16)
        for copy in outs:
            copy.wait()


def core_rows(cube, place, target, source):
    rows, width = source.shape
    piece = width // cube.dp_size
    here = place[0] % 2 == 0
    for slab in range(width // LANES):
        flipped = source[:, slab * LANES : (slab + 1) * LANES].T
        for pair in range(LANES // (2 * piece)):
            at = 2 * pair * piece
            at_target = slab * LANES // 2 + pair * piece
            target[at_target : at_target + piece, :] = jnp.where(
                here, flipped[at : at + piece], flipped[at + piece : at + 2 * piece]
            )


def piece_copies(cube, place, relative, table, outs, sem, first, count):
    dp_at = place[0]
    item = jnp.bitwise_xor(place[1], relative)
    piece = table.shape[1] * 2 // cube.dp_size
    copies = []
    for part, order in enumerate(cube.sum_orders):
        half, rows = outs[2 * part].shape[0], outs[2 * part].shape[1]
        for index in range(2 * half):
            dp_mask, tensor_mask = cube.masks(order, index)
            if tensor_mask != relative:
                continue
            pair = jnp.bitwise_xor(dp_at, dp_mask) // 2
            row = pl.multiple_of(pair * piece + part * rows, 16)
            out = outs[2 * part + index // half]
            copies.append(
                pltpu.make_async_copy(
                    table.at[item, pl.ds(row, rows), :],
                    out.at[index % half, :, pl.ds(first, count)],
                    sem,
                )
            )
    return copies


def wide_grad_kernel(cube, per, place, left, left_far, right, right_far, *refs):
    outs, (flip, table, sem) = refs[:-3], refs[-3:]
    step = pl.program_id(0)
    local, block = table.shape[2], right.shape[1]

    @pl.when(step == 0)
    def _():
        core_rows(cube, place, flip.at[0], left)
        core_rows(cube, place, flip.at[1], left_far)

    got = (dot(flip[0], right[...]) + dot(flip[1], right_far[...])).astype(BF16)
    item = jnp.bitwise_xor(place[1], step // per)
    table[item, :, pl.ds(pl.multiple_of((step % per) * block, LANES), block)] = got
    for relative in range(cube.tensor_size):
        copies = piece_copies(cube, place, relative, table, outs, sem, 0, local)

        @pl.when(step == relative * per + per - 1)
        def _():
            for copy in copies:
                copy.start()

        @pl.when(step == cube.tensor_size * per - 1)
        def _():
            for copy in copies:
                copy.wait()


def qkv_grad_kernel(cube, with_proj, place, mixed, mixed_far, grads, grads_far, *refs):
    if with_proj:
        gated, gated_far, heads, heads_far = refs[:4]
        outs, refs = refs[4:8], refs[8:]
        flip, table, mat, mat_far, own, far, sem, in_sem, small, sides, sides_far = refs
    else:
        outs, refs = refs[:4], refs[4:]
        flip, table, mat, mat_far, own, far, sem, in_sem = refs
    copies = [
        pltpu.make_async_copy(source, target, in_sem.at[place_at])
        for place_at, (source, target) in enumerate(
            ((mixed, mat), (mixed_far, mat_far), (grads, own), (grads_far, far))
        )
    ]
    if with_proj:
        copies += [
            pltpu.make_async_copy(source, target, in_sem.at[4 + place_at])
            for place_at, (source, target) in enumerate(((heads, sides), (heads_far, sides_far)))
        ]
    for copy in copies:
        copy.start()
    local = table.shape[2] // 3
    for copy in copies[:2]:
        copy.wait()
    core_rows(cube, place, flip.at[0], mat)
    core_rows(cube, place, flip.at[1], mat_far)
    if with_proj:
        late = [
            pltpu.make_async_copy(source, target, in_sem.at[place_at])
            for place_at, (source, target) in enumerate(((gated, mat), (gated_far, mat_far)))
        ]
        for copy in late:
            copy.start()
    for copy in copies[2:4]:
        copy.wait()
    started = []
    for relative in range(cube.tensor_size):
        item = jnp.bitwise_xor(place[1], relative)
        cols = pl.ds(pl.multiple_of(item * local, LANES), local)
        for kind in range(3):
            table[item, :, kind * local : (kind + 1) * local] = (
                dot(flip[0], own[kind, :, cols]) + dot(flip[1], far[kind, :, cols])
            ).astype(BF16)
        group = piece_copies(cube, place, relative, table, outs, sem, 0, 3 * local)
        for copy in group:
            copy.start()
        started += group
    if with_proj:
        narrow = small.shape[2]
        for copy in late + copies[4:]:
            copy.wait()
        core_rows(cube, place, flip.at[0], mat)
        core_rows(cube, place, flip.at[1], mat_far)
        for relative in range(cube.tensor_size):
            item = jnp.bitwise_xor(place[1], relative)
            cols = pl.ds(pl.multiple_of(item * narrow, LANES), narrow)
            small[item] = (dot(flip[0], sides[:, cols]) + dot(flip[1], sides_far[:, cols])).astype(
                BF16
            )
            group = piece_copies(cube, place, relative, small, outs, sem, 3 * local, narrow)
            for copy in group:
                copy.start()
            started += group
    for copy in started:
        copy.wait()


def split_into(base, lanes, start, values):
    high = values.astype(BF16)
    rest = (values - high.astype(F32)).astype(BF16)
    base = jnp.where(lanes == start, high, base)
    return jnp.where(lanes == start + 1, rest, base)


def attend_back_kernel(
    query, key, value, grad, log_sum, r_query, r_key, head_scale, query_code, key_code,
    grads, sums, flat_query, sides, pairs,
):
    rows = query.shape[0]
    step = pairs.shape[1] // 2
    lanes = lane_index(rows)
    low = lanes < HEAD
    inner = lanes % HEAD
    q, k, v, g = query[...], key[...], value[...], grad[...]
    ones = head_ones()
    spare = 16
    zero = jnp.zeros((rows, LANES), BF16)
    one = jnp.ones((rows, LANES), BF16)
    marks = (inner == spare) | (inner == spare + 1)

    @pl.when(pl.program_id(0) == 0)
    def _():
        pairs[...] = jnp.zeros_like(pairs)
        sides[...] = jnp.zeros_like(sides)

    qc = split_into(query_code[...], inner, spare, -log_sum[...])
    high = jnp.logical_not(low)
    q_wide = jnp.concatenate([q, qc], axis=1)
    for head in range(2):
        side = low if head == 0 else high
        k_code = jnp.where(marks & (high if head == 0 else low), one, key_code[...])
        k_side = jnp.where(side, k, zero)
        k_wide = jnp.concatenate([k_side, k_code], axis=1)
        v_side = jnp.where(side, v, zero)
        at = slice(head * step, head * step + rows)
        sides[0, at, :] = jnp.where(side, g, zero)
        sides[1, at, :] = jnp.where(side, q, zero)
        probs = jnp.exp(dot_nt(k_wide, q_wide))
        pairs[0:rows, at] = probs.astype(BF16)
        weighted = probs * dot_nt(v_side, g)
        change = (weighted - probs * jnp.sum(weighted, axis=0, keepdims=True)).astype(BF16)
        pairs[step : step + rows, at] = change
        flat = dot(k_side.T, change)
        if head == 0:
            flat_query[...] = flat
        else:
            flat_query[...] += flat
    d_value = dot(pairs[0:rows, :], sides[0]).astype(BF16)
    d_key = dot(pairs[step : step + rows, :], sides[1])
    d_query = flat_query[...].T
    scale = head_scale[0:1, :]
    unit = q.astype(F32) / scale
    along = head_sums(unit * d_query, ones)
    out = (r_query[...] * scale * (d_query - unit * along)).astype(BF16)
    grads[0] = out
    sums[0:1, :] = jnp.sum(out.astype(F32), axis=0, keepdims=True)
    sums[2:3, :] = jnp.sum(along, axis=0, keepdims=True)
    unit_key = k.astype(F32)
    along_key = head_sums(unit_key * d_key, ones)
    grads[1] = (r_key[...] * (d_key - unit_key * along_key)).astype(BF16)
    grads[2] = d_value
    sums[1:2, :] = jnp.sum(d_value.astype(F32), axis=0, keepdims=True)


def last_kernel(cube, splits, place, modul, tokens, g_middle, *refs):
    held, refs = refs[:8], refs[8:]
    grads, refs = refs[: len(splits)], refs[len(splits) :]
    grad_tokens, sums, weight, left, tokens_here, middle_here, sem, in_sem = refs[:8]
    grads_here = refs[8:]
    rows, width = tokens_here.shape
    local = width // cube.tensor_size
    copies = [
        pltpu.make_async_copy(source, target, in_sem.at[place_at])
        for place_at, (source, target) in enumerate(
            list(zip(grads, grads_here)) + [(tokens, tokens_here), (g_middle, middle_here)]
        )
    ]
    for copy in copies:
        copy.start()
    pieces = make_pieces(cube, place, held, (0, weight.shape[2]), weight, sem)
    for copy in pieces:
        copy.start()
    for which, (start, size) in enumerate(splits):
        copies[which].wait()
        for item in range(cube.tensor_size):
            for kind in range(3):
                at = kind * local + start
                left[item, :, at : at + size] = grads_here[which][
                    kind, :, item * size : (item + 1) * size
                ]
    for copy in copies[len(splits) :] + pieces:
        copy.wait()
    gain = 1.0 + modul[2:3, :]
    totals = [jnp.zeros((1, width), F32) for _ in range(2)]
    for first, count in row_chunks(rows, 352):
        out = dot_nt(left[0, first : first + count, :], weight[0])
        for item in range(1, cube.tensor_size):
            out = out + dot_nt(left[item, first : first + count, :], weight[item])
        for inner, inner_count in row_chunks(count, 64):
            at = slice(first + inner, first + inner + inner_count)
            grad = out[inner : inner + inner_count]
            centred, scale = moments(tokens_here[at, :].astype(F32))
            normed = centred * scale
            totals[0] += jnp.sum(grad * normed, axis=0, keepdims=True)
            totals[1] += jnp.sum(grad, axis=0, keepdims=True)
            lifted = grad * gain
            back = middle_here[at, :] + scale * (
                lifted
                - jnp.mean(lifted, axis=-1, keepdims=True)
                - normed * jnp.mean(lifted * normed, axis=-1, keepdims=True)
            )
            grad_tokens[at, :] = back.astype(BF16)
    for place_at in range(2):
        sums[place_at : place_at + 1, :] = totals[place_at]


def pack_kernel(splits, sums_one, gamma_sum, sums_zero, fc1_bias_sum, gated_sum, *refs):
    parts, (out, side) = refs[: len(splits)], refs[len(splits) :]
    dp_size = side.shape[0]
    tensor_size = out.shape[0] // dp_size
    width = gamma_sum.shape[1]
    local, wide = width // tensor_size, fc1_bias_sum.shape[1] // tensor_size
    owners = LANES * dp_size // width
    for slab in range(width // LANES):
        cols = slice(slab * LANES, (slab + 1) * LANES)
        rows = slice(slab * owners, (slab + 1) * owners)
        side[rows, 0:LANES] = jnp.broadcast_to(gated_sum[:, cols], (owners, LANES))
        side[rows, LANES : 2 * LANES] = jnp.broadcast_to(sums_one[3:4, cols], (owners, LANES))
    modul = (
        sums_one[2:3, :], gamma_sum[...], sums_zero[0:1, :],
        sums_one[0:1, :], sums_zero[1:2, :], sums_one[1:2, :],
    )
    for item in range(tensor_size):
        rows = slice(item * dp_size, (item + 1) * dp_size)

        def put(at, values):
            count = values.shape[1]
            out[rows, at : at + count] = jnp.broadcast_to(values, (dp_size, count)).astype(BF16)

        for kind, values in enumerate(modul):
            put(kind * local, values[:, item * local : (item + 1) * local])
        for kind in range(3):
            for part, (start, size) in zip(parts, splits):
                at = (6 + kind) * local + start
                values = part[kind : kind + 1, item * size : (item + 1) * size]
                put(at, values)
                if kind == 2:
                    put(at + local, values - values.astype(BF16).astype(F32))
        put(10 * local, fc1_bias_sum[:, item * wide : (item + 1) * wide])
        out[rows, 10 * local + wide :] = side[...].astype(BF16)


def add_kernel(parts, groups, merge, *refs):
    outs = refs[4 * parts * groups :]
    at = 0
    for part in range(parts):
        first = 0
        for group in range(groups):
            for side in range(2):
                kept, received = refs[at], refs[at + 1]
                at += 2
                rows, count = kept.shape[1:]
                total = (kept[...].astype(F32) + received[...].astype(F32)).astype(BF16)
                base = part * rows if merge else 0
                out = outs[side] if merge else outs[2 * part + side]
                out[:, base : base + rows, first : first + count] = total
            first += count


def add_pieces(kept, received, merge):
    groups, parts = len(kept), len(kept[0])
    items, rows = kept[0][0].shape[0], kept[0][0].shape[1]
    half = items // 2
    per = max(1, half // 2)
    columns = sum(group[0].shape[2] for group in kept)
    operands, specs = [], []
    for part in range(parts):
        for group in range(groups):
            block = (per, rows, kept[group][part].shape[2])
            for side in range(2):
                spec = pl.BlockSpec(block, lambda i, side=side: (i + side * (half // per), 0, 0))
                operands += [kept[group][part], received[group][part]]
                specs += [spec, spec]
    out_rows, out_parts = (parts * rows, 1) if merge else (rows, parts)
    return pl.pallas_call(
        functools.partial(add_kernel, parts, groups, merge),
        out_shape=[jax.ShapeDtypeStruct((half, out_rows, columns), BF16)] * (2 * out_parts),
        grid=(half // per,),
        in_specs=specs,
        out_specs=[pl.BlockSpec((per, out_rows, columns), lambda i: (i, 0, 0))] * (2 * out_parts),
        cost_estimate=pl.CostEstimate(flops=1 << 20, bytes_accessed=1 << 20, transcendentals=0),
        compiler_params=pltpu.CompilerParams(vmem_limit_bytes=VMEM_BYTES),
        name="add",
    )(*operands)


def scale_codes(lengths, rows):
    count = lengths.shape[0]
    bounds = jnp.cumsum(lengths)
    places = jnp.arange(rows, dtype=jnp.int32)
    scale_of = jnp.sum((places[:, None] >= bounds[None, :]).astype(jnp.int32), axis=1)
    lane = jnp.arange(HEAD, dtype=jnp.int32)
    query_code = (scale_of[:, None] == lane[None, :]).astype(BF16)
    blocked = (scale_of[:, None] > lane[None, :]) & (lane[None, :] < count)
    key_code = jnp.where(blocked, MASKED, 0.0).astype(BF16)
    return jnp.tile(query_code, (1, 2)), jnp.tile(key_code, (1, 2))


def to_all(values, axes=AXES):
    return lax.all_to_all(values, axes, split_axis=0, concat_axis=0, tiled=True)


def local(
    tokens, condition, scale_lens, qkv_weight, qv_bias, head_scale, proj_weight, proj_bias,
    fc1_weight, fc1_bias, fc2_weight, fc2_bias, ada_weight, ada_bias, cotangent,
):
    dp_size, tensor_size = lax.axis_size("dp"), lax.axis_size("tensor")
    devices = dp_size * tensor_size
    cube = Cube(dp_size, tensor_size)
    dp_at, tensor_at = lax.axis_index("dp"), lax.axis_index("tensor")
    place = jnp.stack([dp_at, tensor_at]).astype(jnp.int32)
    rows, width = tokens.shape
    piece_rows = qkv_weight.shape[0]
    narrow = qkv_weight.shape[2]
    wide = fc1_weight.shape[1]
    hidden_width = wide * tensor_size

    cond_float = condition.astype(F32)
    cond_low = jax.nn.silu(cond_float).astype(BF16)
    cond_parts = cond_low.reshape(tensor_size, dp_size, piece_rows).transpose(1, 0, 2)
    cond_own = lax.all_to_all(cond_parts, "dp", split_axis=0, concat_axis=0, tiled=True)
    cond_back = cond_own.reshape(dp_size, tensor_size, piece_rows).transpose(1, 0, 2)
    cond_back = cond_back.reshape(devices, piece_rows)
    cond_own = cond_own.reshape(devices, piece_rows)
    ada_flat = ada_weight.reshape(piece_rows, 6 * narrow)

    narrow_gather = Gather(
        cube,
        jnp.concatenate([qkv_weight.reshape(piece_rows, 3 * narrow), proj_weight.T], axis=1),
    )
    narrow_gather.advance(cond_own)
    wide_shard = jnp.concatenate([fc1_weight, fc2_weight.T], axis=1)
    wide_all = lax.all_gather(
        behind(wide_shard, narrow_gather.held), AXES, axis=0, tiled=True
    ).reshape(dp_size, tensor_size, piece_rows, 2 * wide)
    while narrow_gather.step < cube.hops - 2:
        narrow_gather.advance()

    modul_part = jnp.dot(cond_own, ada_flat, preferred_element_type=F32)
    bias_part = jnp.where(dp_at == 0, ada_bias.astype(F32).reshape(1, 6 * narrow), 0.0)
    dp_part = jnp.concatenate([proj_bias, fc2_bias]).astype(F32)
    tensor_part = jnp.concatenate(
        [qv_bias.astype(F32).reshape(-1), jnp.repeat(head_scale, HEAD), fc1_bias.astype(F32)]
    )
    share = -(-tensor_part.shape[0] // (dp_size * LANES)) * LANES
    pieces = tensor_part.shape[0] // share
    tensor_share = lax.dynamic_index_in_dim(
        tensor_part.reshape(pieces, share), jnp.minimum(dp_at, pieces - 1), 0, keepdims=False
    )
    rest = jnp.concatenate([dp_part, tensor_share])[None]
    parts = to_all(
        jnp.concatenate(
            [modul_part + bias_part, jnp.broadcast_to(rest, (devices, rest.shape[1]))], axis=1
        )
    ).reshape(dp_size, tensor_size, -1)
    held = narrow_gather.sides(parts)
    rest = parts[:, 0, 6 * narrow :]
    proj_bias_full = rest[:, :piece_rows].reshape(1, width)
    fc2_bias_full = rest[:, piece_rows : 2 * piece_rows].reshape(1, width)

    own_lens = lax.dynamic_index_in_dim(scale_lens, tensor_at, 0, keepdims=False)
    query_code, key_code = scale_codes(own_lens, rows)

    dma = pltpu.SemaphoreType.DMA

    def half_shape(*dims):
        return shape(*dims, dtype=BF16)

    mixed_one, query, key, value, r_query, r_key, modul, fc1_bias_full, head_scale_full = call(
        functools.partial(front_kernel, cube, pieces),
        [half_shape(rows, width)] * 4
        + [shape(rows, width)] * 2
        + [shape(8, width), shape(1, hidden_width), shape(1, width)],
        [SMEM, VMEM, VMEM] + [ANY] * 8,
        [VMEM] * 9,
        [
            pltpu.VMEM((tensor_size, width, 3 * narrow), BF16),
            dma,
            pltpu.VMEM((2, width), F32),
        ],
        16, "front",
    )(place, tokens, parts, *held)
    mixed_one_far = cube.hop(mixed_one, cube.core)

    slab = pl.BlockSpec((rows, LANES), lambda i: (0, i))
    whole = pl.BlockSpec((rows, LANES), lambda i: (0, 0))
    heads, log_sum = call(
        attend_kernel,
        [half_shape(rows, width), shape(rows, width)],
        [slab] * 3 + [whole] * 2,
        [slab] * 2,
        [],
        20, "attend", grid=(width // LANES,),
    )(query, key, value, query_code, key_code)
    heads_far = cube.hop(heads, cube.core)

    branch, middle, mixed_two, gated_sum = call(
        functools.partial(middle_kernel, cube),
        [shape(rows, width)] * 2 + [half_shape(2, rows, width), shape(1, width)],
        [SMEM] + [VMEM] * 5 + [ANY] * 8,
        [VMEM] * 4,
        [pltpu.VMEM((tensor_size, width, narrow), BF16), dma],
        10, "middle", after=[mixed_one_far],
    )(place, heads, tokens, cotangent, modul, proj_bias_full, *held)
    mixed_two_far = cube.hop(mixed_two, cube.core)

    block = min(1024, wide)
    per = wide // block
    wide_steps = tensor_size * per

    def wide_block(first):
        return pl.BlockSpec(
            (dp_size, None, piece_rows, block), lambda i: (0, i // per, 0, first * per + i % per)
        )

    side = pl.BlockSpec((rows, block), lambda i: (0, i))
    side_row = pl.BlockSpec((1, block), lambda i: (0, i))

    def mixed_part(which):
        return pl.BlockSpec((None, rows, width), lambda i: (which, 0, 0))

    hidden, slope = call(
        hidden_kernel,
        [half_shape(rows, hidden_width), shape(rows, hidden_width)],
        [mixed_part(0), side_row, wide_block(0)],
        [side] * 2,
        [],
        20, "hidden", grid=(wide_steps,), after=[heads_far],
    )(mixed_two, fc1_bias_full, wide_all)
    hidden_far = cube.hop(hidden, cube.core)

    grad_pre, fc1_bias_sum = call(
        pre_back_kernel,
        [half_shape(rows, hidden_width), shape(1, hidden_width)],
        [side, mixed_part(1), wide_block(1)],
        [side, side_row],
        [],
        300, "pre_back", grid=(wide_steps,), after=[mixed_two_far],
    )(slope, mixed_two, wide_all)
    grad_pre_far = cube.hop(grad_pre, cube.core)

    def piece_shapes(columns):
        return [half_shape(devices // 4, piece_rows // 2, columns)] * 4

    def pairs(outs):
        return list(zip(outs[0::2], outs[1::2]))

    flip_scratch = pltpu.VMEM((2, width // 2, rows), BF16)
    grad_scratch = [flip_scratch, pltpu.VMEM((tensor_size, width // 2, wide), BF16), dma]

    def mixed_far_part(which):
        return pl.BlockSpec((None, rows, width), lambda i, at: (which, 0, 0))

    side_relative = pl.BlockSpec(
        (rows, block), lambda i, at: (0, jnp.bitwise_xor(at[1], i // per) * per + i % per)
    )

    def wide_grad(which, right, right_far, name, after):
        return call(
            functools.partial(wide_grad_kernel, cube, per),
            piece_shapes(wide),
            [mixed_far_part(which)] * 2 + [side_relative] * 2,
            [ANY] * 4,
            grad_scratch,
            300, name, grid=(wide_steps,), after=after, scalars=1,
        )(place, mixed_two, mixed_two_far, right, right_far)

    outs = wide_grad(1, hidden, hidden_far, "fc2_grad", [grad_pre])
    fc2_sum = Scatter(cube, [pairs(outs)])
    outs = wide_grad(0, grad_pre, grad_pre_far, "fc1_grad", [outs[0]])
    fc1_sum = Scatter(cube, [pairs(outs)])

    full = pltpu.VMEM((rows, width), F32)
    full_half = pltpu.VMEM((rows, width), BF16)
    whole_row = pl.BlockSpec((1, width), lambda i: (0, 0))
    eight_rows = pl.BlockSpec((8, width), lambda i: (0, 0))
    whole_half = pl.BlockSpec((rows, width), lambda i: (0, 0))
    g_middle, gated_one, g_heads, sums_one = call(
        functools.partial(first_back_kernel, cube, wide_steps),
        [
            shape(rows, width),
            half_shape(rows, width),
            half_shape(rows, width),
            shape(8, width),
        ],
        [SMEM, side, wide_block(0)] + [ANY] * 3 + [eight_rows] + [ANY] * 8,
        [ANY, ANY, whole_half, eight_rows],
        [
            full, full, full, full_half, full_half,
            pltpu.VMEM((tensor_size, width, narrow), BF16),
            dma((3,)), dma,
        ],
        500, "first_back", grid=(wide_steps,), after=[outs[0]],
    )(place, grad_pre, wide_all, middle, branch, cotangent, modul, *held)
    gated_one_far = cube.hop(gated_one, cube.core)

    splits = [(0, narrow // 2), (narrow // 2, narrow // 2)]
    if narrow < 2 * LANES:
        splits = [(0, narrow)]
    steps = narrow // LANES
    padded = -(-rows // LANES) * LANES

    def attend_back(start, size, after):
        per, base = size // LANES, start // LANES

        def column(i):
            return (i // per) * steps + base + i % per

        picked = pl.BlockSpec((rows, LANES), lambda i: (0, column(i)))
        picked_row = pl.BlockSpec((1, LANES), lambda i: (0, column(i)))
        count = tensor_size * per
        return call(
            attend_back_kernel,
            [half_shape(3, rows, count * LANES), shape(8, count * LANES)],
            [picked] * 7 + [picked_row] + [whole] * 2,
            [
                pl.BlockSpec((3, rows, LANES), lambda i: (0, 0, i)),
                pl.BlockSpec((8, LANES), lambda i: (0, i)),
            ],
            [
                pltpu.VMEM((LANES, rows), F32),
                pltpu.VMEM((2, 2 * padded, LANES), BF16),
                pltpu.VMEM((2 * padded, 2 * padded), BF16),
            ],
            400, "attend_back", grid=(count,), after=after,
        )(query, key, value, g_heads, log_sum, r_query, r_key, head_scale_full,
          query_code, key_code)

    def qkv_grad(size, with_proj, grads, grads_far, after):
        extra = [gated_one, gated_one_far, heads, heads_far] if with_proj else []
        cut = pltpu.VMEM((3, rows, tensor_size * size), BF16)
        proj_scratch = [pltpu.VMEM((tensor_size, width // 2, narrow), BF16), full_half, full_half]
        return call(
            functools.partial(qkv_grad_kernel, cube, with_proj),
            piece_shapes(3 * size + (narrow if with_proj else 0)),
            [SMEM] + [ANY] * (4 + len(extra)),
            [ANY] * 4,
            [
                flip_scratch,
                pltpu.VMEM((tensor_size, width // 2, 3 * size), BF16),
                full_half, full_half, cut, cut,
                dma, dma((6,)),
            ] + (proj_scratch if with_proj else []),
            200, "qkv_grad", after=after,
        )(place, mixed_one, mixed_one_far, grads, grads_far, *extra)

    after = fc2_sum.advance(sums_one)
    qkv_grads, qkv_grads_far, all_sums = [], [], []
    for start, size in splits:
        grads, part_sums = attend_back(start, size, after)
        qkv_grads.append(grads)
        all_sums.append(part_sums)
        qkv_grads_far.append(cube.hop(grads, cube.core))
        after = [grads] + fc2_sum.advance(part_sums) + fc1_sum.advance(part_sums)
        if len(all_sums) == 1:
            after += [gated_one_far]
    qkv_sum = Scatter(cube, [])
    for which, (start, size) in enumerate(splits):
        outs = qkv_grad(size, which == 0, qkv_grads[which], qkv_grads_far[which], after)
        qkv_sum.add(pairs(outs))
        after = [outs[0]]
    fc2_received = fc2_sum.received
    after += fc1_sum.advance(outs[0])
    output, gamma_sum = call(
        functools.partial(output_kernel, wide_steps),
        [half_shape(rows, width), shape(1, width)],
        [side, wide_block(1)] + [ANY] * 2 + [eight_rows, whole_row],
        [whole_half, whole_row],
        [full, full_half, full, dma((2,))],
        400, "output", grid=(wide_steps,), after=after + [fc2_received[0][0]],
    )(hidden, wide_all, cotangent, middle, modul, fc2_bias_full)
    fc1_received = fc1_sum.received
    after = qkv_sum.advance(gamma_sum) + [fc1_received[0][0]]
    grad_tokens, sums_zero = call(
        functools.partial(last_kernel, cube, splits),
        [half_shape(rows, width), shape(8, width)],
        [SMEM, VMEM] + [ANY] * (10 + len(splits)),
        [VMEM] * 2,
        [
            pltpu.VMEM((tensor_size, width, 3 * narrow), BF16),
            pltpu.VMEM((tensor_size, rows, 3 * narrow), BF16),
            full_half, full, dma, dma((2 + len(splits),)),
        ]
        + [pltpu.VMEM((3, rows, tensor_size * size), BF16) for start, size in splits],
        400, "last", after=after,
    )(place, modul, tokens, g_middle, *held, *qkv_grads)

    near_out = qkv_sum.advance(sums_zero)

    late = call(
        functools.partial(pack_kernel, splits),
        half_shape(devices, 10 * narrow + wide + 2 * LANES),
        [VMEM] * (5 + len(splits)),
        VMEM,
        [pltpu.VMEM((dp_size, 2 * LANES), F32)],
        1, "pack",
    )(sums_one, gamma_sum, behind(sums_zero, near_out), fc1_bias_sum, gated_sum, *all_sums)
    far_out = qkv_sum.advance(late)
    late = behind(to_all(late, BACK_AXES), far_out)
    fc2_own = fc2_sum.finish(far_out)
    fc1_own = fc1_sum.finish(far_out)
    grad_modul_all = late[:, : 6 * narrow]
    late_sum = jnp.sum(late.astype(F32), axis=0)
    grad_ada_bias = late_sum[: 6 * narrow].reshape(6, narrow)
    grad_qv_bias = late_sum[6 * narrow : 8 * narrow].reshape(2, narrow)
    head_sum = late_sum[8 * narrow : 9 * narrow] + late_sum[9 * narrow : 10 * narrow]
    grad_head_scale = head_sum.reshape(-1, HEAD)[:, 0]
    rest = late_sum[10 * narrow :]
    grad_fc1_bias = rest[:wide]
    first_own = (dp_at % (LANES // piece_rows)) * piece_rows
    own_rows = lax.dynamic_slice_in_dim(rest[wide:].reshape(2, LANES), first_own, piece_rows, axis=1)
    grad_fc2_bias, grad_proj_bias = own_rows[0], own_rows[1]
    grad_ada = lax.dot_general(
        cond_back, grad_modul_all, (((0,), (0,)), ((), ())), preferred_element_type=F32
    ).reshape(piece_rows, 6, narrow)
    cond_part = dot_nt(grad_modul_all, ada_flat)
    cond_all = to_all(cond_part, BACK_AXES).reshape(tensor_size, dp_size, piece_rows)
    own = qkv_sum.finish(cond_part)
    parts_own, first = [], 0
    for which, (start, size) in enumerate(splits):
        parts_own.append(own[:, first : first + 3 * size].reshape(piece_rows, 3, size))
        first += 3 * size
        if which == 0:
            proj_own = own[:, first : first + narrow].T
            first += narrow
    qkv_own = jnp.concatenate(parts_own, axis=2)

    cond_image = lax.dynamic_slice_in_dim(cond_float, tensor_at, 1, axis=0)
    unused, silu_back = jax.vjp(jax.nn.silu, cond_image)
    grad_condition = silu_back(jnp.sum(cond_all, axis=0).reshape(1, width))[0]

    return (
        output,
        grad_tokens,
        grad_condition,
        qkv_own,
        grad_qv_bias,
        grad_head_scale,
        proj_own,
        grad_proj_bias,
        fc1_own,
        grad_fc1_bias,
        fc2_own.T,
        grad_fc2_bias,
        grad_ada,
        grad_ada_bias,
    )


def solution(mesh):
    return jax.shard_map(
        local,
        mesh=mesh,
        in_specs=(
            P(("dp", "tensor"), None),
            P("dp", None),
            P("dp", None),
            P("dp", None, "tensor"),
            P(None, "tensor"),
            P("tensor"),
            P("tensor", "dp"),
            P("dp"),
            P("dp", "tensor"),
            P("tensor"),
            P("tensor", "dp"),
            P("dp"),
            P("dp", None, "tensor"),
            P(None, "tensor"),
            P(("dp", "tensor"), None),
        ),
        out_specs=(
            P(("dp", "tensor"), None),
            P(("dp", "tensor"), None),
            P(("dp", "tensor"), None),
            P("dp", None, "tensor"),
            P(None, "tensor"),
            P("tensor"),
            P("tensor", "dp"),
            P("dp"),
            P("dp", "tensor"),
            P("tensor"),
            P("tensor", "dp"),
            P("dp"),
            P("dp", None, "tensor"),
            P(None, "tensor"),
        ),
        check_vma=False,
    )
```

```python
import functools

import jax
import jax.numpy as jnp
from jax import lax
from jax.experimental import pallas as pl
from jax.experimental.pallas import tpu as pltpu
from jax.sharding import PartitionSpec as P

SEQ = 680
NORM_EPS = 1e-06
HEAD_EPS = 1e-06
MASKED = -1e30
HEAD = 64
LANES = 128
GELU_C = 0.7978845608
GELU_A = 0.044715
AXES = ("dp", "tensor")
BACK_AXES = ("tensor", "dp")
VMEM_BYTES = 56 * 1024 * 1024

F32 = jnp.float32
BF16 = jnp.bfloat16
VMEM = pl.BlockSpec(memory_space=pltpu.VMEM)
SMEM = pl.BlockSpec(memory_space=pltpu.SMEM)
ANY = pl.BlockSpec(memory_space=pl.ANY)


def dot(left, right):
    return lax.dot_general(left, right, (((1,), (0,)), ((), ())), preferred_element_type=F32)


def dot_nt(left, right):
    return lax.dot_general(left, right, (((1,), (1,)), ((), ())), preferred_element_type=F32)


def row_chunks(rows, size):
    return [(first, min(size, rows - first)) for first in range(0, rows, size)]


def call(
    kernel, out_shape, in_specs, out_specs, scratch, cost, name, grid=None, after=(), scalars=0
):
    count = len(in_specs) + scalars
    in_specs = list(in_specs) + [ANY] * len(after)
    if scalars:
        extra = {
            "grid_spec": pltpu.PrefetchScalarGridSpec(
                num_scalar_prefetch=scalars,
                grid=grid,
                in_specs=in_specs,
                out_specs=out_specs,
                scratch_shapes=scratch,
            )
        }
    else:
        extra = {"in_specs": in_specs, "out_specs": out_specs, "scratch_shapes": scratch}
        if grid is not None:
            extra["grid"] = grid

    def body(*refs):
        kernel(*refs[:count], *refs[count + len(after) :])

    run = pl.pallas_call(
        body,
        out_shape=out_shape,
        cost_estimate=pl.CostEstimate(
            flops=int(cost * 1e9), bytes_accessed=1 << 20, transcendentals=0
        ),
        compiler_params=pltpu.CompilerParams(vmem_limit_bytes=VMEM_BYTES),
        name=name,
        **extra,
    )
    return lambda *operands: run(*operands, *after)


def shape(*dims, dtype=F32):
    return jax.ShapeDtypeStruct(dims, dtype)


class Cube:
    def __init__(self, dp_size, tensor_size):
        self.dp_size, self.tensor_size = dp_size, tensor_size
        dp_bits = dp_size.bit_length() - 1
        tensor_bits = tensor_size.bit_length() - 1
        far = [("dp", 1 << bit) for bit in range(2, dp_bits)]
        near = [("dp", 2)]
        side = [("tensor", 1 << bit) for bit in reversed(range(tensor_bits))]
        core = [("dp", 1)]
        self.orders = (core + side + near + far, core + near + side + far)
        self.sum_orders = (side + near + far, near + side + far)
        self.near_hops = len(side) + 1
        self.core = core[0]
        self.devices = dp_size * tensor_size

    def hop(self, values, hop):
        axis, mask = hop
        size = self.dp_size if axis == "dp" else self.tensor_size
        return lax.ppermute(values, axis, [(i, i ^ mask) for i in range(size)])

    def masks(self, order, index):
        dp_mask, tensor_mask = 0, 0
        for place, (axis, mask) in enumerate(order):
            if (index >> (len(order) - 1 - place)) & 1:
                if axis == "dp":
                    dp_mask |= mask
                else:
                    tensor_mask |= mask
        return dp_mask, tensor_mask

    def index(self, order, dp_rel, tensor_rel):
        total = 0
        for place, (axis, mask) in enumerate(order):
            rel = dp_rel if axis == "dp" else tensor_rel
            bit = (rel // mask) % 2
            total = total + bit * (1 << (len(order) - 1 - place))
        return total

    @property
    def hops(self):
        return len(self.orders[0])


def behind(values, others):
    kept, unused = lax.optimization_barrier((values, others))
    return kept


class Gather:
    def __init__(self, cube, shard):
        self.cube = cube
        rows = shard.shape[0] // 2
        self.step = 0
        self.held = [shard[None, :rows], shard[None, rows:]]
        self.launch()

    def launch(self):
        hops = [order[len(order) - 1 - self.step] for order in self.cube.orders]
        self.received = [self.cube.hop(held, hop) for held, hop in zip(self.held, hops)]

    def advance(self, others=None):
        if others is not None:
            self.received = behind(self.received, others)
        self.step += 1
        self.held = [jnp.concatenate(pair, axis=0) for pair in zip(self.held, self.received)]
        self.launch()

    def sides(self, others=None):
        crossed = [self.cube.hop(held, self.cube.core) for held in self.held]
        if others is not None:
            self.received = behind(self.received, others)
        got = []
        for held, received, other in zip(self.held, self.received, crossed):
            got += [held, received, other, self.cube.hop(received, self.cube.core)]
        return got


class Scatter:
    def __init__(self, cube, groups):
        self.cube, self.step = cube, 0
        self.kept, self.received = [], []
        for group in groups:
            self.add(group)

    def add(self, pairs):
        self.kept.append([keep for keep, send in pairs])
        self.received.append(self.launch([send for keep, send in pairs]))

    def launch(self, outgoing):
        return [
            self.cube.hop(values, order[self.step])
            for values, order in zip(outgoing, self.cube.sum_orders)
        ]

    def advance(self, others=None):
        if self.step == self.cube.hops - 2:
            return []
        if others is not None:
            self.received = behind(self.received, others)
        self.step += 1
        merge = self.step >= self.cube.near_hops
        outs = add_pieces(self.kept, self.received, merge)
        self.kept = [list(outs[0::2])]
        if merge:
            self.received = [[self.cube.hop(outs[1], self.cube.sum_orders[0][self.step])]]
        else:
            self.received = [self.launch(outs[1::2])]
        return list(outs)

    def finish(self, others=None):
        while self.step < self.cube.hops - 2:
            self.advance()
        received = self.received if others is None else behind(self.received, others)
        return self.kept[0][0][0].astype(F32) + received[0][0][0].astype(F32)


def start_pieces(cube, place, held, columns, target, sem):
    copies = make_pieces(cube, place, held, columns, target, sem)
    for copy in copies:
        copy.start()
    return copies


def make_pieces(cube, place, held, columns, target, sem):
    dp_at, tensor_at = place[0], place[1]
    first, count = columns
    quarter = cube.devices // 4
    copies = []
    for part, order in enumerate(cube.orders):
        for side in range(4):
            source = held[4 * part + side]
            rows = source.shape[1]
            for item in range(quarter):
                dp_mask, tensor_mask = cube.masks(order, side * quarter + item)
                owner = jnp.bitwise_xor(dp_at, dp_mask)
                tensor_owner = jnp.bitwise_xor(tensor_at, tensor_mask)
                row = pl.multiple_of(owner * (2 * rows) + part * rows, 16)
                copies.append(
                    pltpu.make_async_copy(
                        source.at[item, :, pl.ds(first, count)],
                        target.at[tensor_owner, pl.ds(row, rows), :],
                        sem,
                    )
                )
    return copies


def moments(values):
    average = jnp.mean(values, axis=-1, keepdims=True)
    centred = values - average
    variance = jnp.mean(centred * centred, axis=-1, keepdims=True)
    return centred, lax.rsqrt(variance + NORM_EPS)


def head_ones(lanes=LANES):
    row = lax.broadcasted_iota(jnp.int32, (lanes, lanes), 0) // HEAD
    col = lax.broadcasted_iota(jnp.int32, (lanes, lanes), 1) // HEAD
    return (row == col).astype(BF16)


def head_sums(values, ones):
    high = values.astype(BF16)
    low = (values - high.astype(F32)).astype(BF16)
    return dot(high, ones) + dot(low, ones)


def front_kernel(
    cube, pieces, place, tokens, parts, h0, h1, h2, h3, h4, h5, h6, h7,
    mixed, query, key, value, r_query, r_key, modul, fc1_bias, head_scale,
    weight, sem, qv_bias,
):
    copies = start_pieces(cube, place, (h0, h1, h2, h3, h4, h5, h6, h7), (0, weight.shape[2]), weight, sem)
    rows, width = tokens.shape
    local = width // cube.tensor_size
    wide = fc1_bias.shape[1] // cube.tensor_size
    share = (3 * local + wide) // pieces
    last = parts.shape[2] - share
    for item in range(cube.tensor_size):
        for kind in range(6):
            at = slice(kind * local, (kind + 1) * local)
            total = parts[0, item : item + 1, at]
            for source in range(1, cube.dp_size):
                total = total + parts[source, item : item + 1, at]
            modul[kind : kind + 1, item * local : (item + 1) * local] = total
        for piece in range(pieces):
            for step in range(0, share, LANES):
                at = piece * share + step
                got = parts[piece, item : item + 1, last + step : last + step + LANES]
                kind, inner = at // local, at % local
                if kind < 2:
                    qv_bias[kind : kind + 1, pl.ds(item * local + inner, LANES)] = got
                elif kind == 2:
                    head_scale[0:1, pl.ds(item * local + inner, LANES)] = got
                else:
                    fc1_bias[0:1, pl.ds(item * wide + at - 3 * local, LANES)] = got
    modul[6:8, :] = jnp.zeros((2, width), F32)
    gain = 1.0 + modul[2:3, :]
    shift = modul[4:5, :]
    for first, count in row_chunks(rows, 64):
        centred, scale = moments(tokens[first : first + count, :].astype(F32))
        mixed[first : first + count, :] = (centred * scale * gain + shift).astype(BF16)
    for copy in copies:
        copy.wait()
    ones = head_ones()
    for item in range(cube.tensor_size):
        for kind in range(3):
            out = dot(mixed[...], weight[item, :, kind * local : (kind + 1) * local])
            for slab in range(local // LANES):
                at = item * local + slab * LANES
                cols = slice(at, at + LANES)
                part = out[:, slab * LANES : (slab + 1) * LANES]
                if kind == 0:
                    part = part + qv_bias[0:1, cols]
                if kind == 2:
                    value[:, cols] = (part + qv_bias[1:2, cols]).astype(BF16)
                    continue
                inverse = lax.rsqrt(head_sums(part * part, ones) + HEAD_EPS)
                unit = part * inverse
                if kind == 0:
                    query[:, cols] = (unit * head_scale[0:1, cols]).astype(BF16)
                    r_query[:, cols] = inverse
                else:
                    key[:, cols] = unit.astype(BF16)
                    r_key[:, cols] = inverse


def lane_index(rows):
    return lax.broadcasted_iota(jnp.int32, (rows, LANES), 1)


def attend_kernel(query, key, value, query_code, key_code, heads, log_sum):
    rows = query.shape[0]
    low = lane_index(rows) < HEAD
    q, k, v = query[...], key[...], value[...]
    qc, kc = query_code[...], key_code[...]
    zero = jnp.zeros_like(v)
    keys = (jnp.where(low, k, kc), jnp.where(low, kc, k))
    queries = (jnp.where(low, q, qc), jnp.where(low, qc, q))
    values = (jnp.where(low, v, zero), jnp.where(low, zero, v))
    for first, count in row_chunks(rows, 352):
        at = slice(first, first + count)
        out, logs = jnp.zeros((count, LANES), F32), []
        for head in range(2):
            expo = jnp.exp(dot_nt(queries[head][at], keys[head]))
            total = jnp.sum(expo, axis=1, keepdims=True)
            out = out + dot((expo * (1.0 / total)).astype(BF16), values[head])
            logs.append(jnp.log(total))
        heads[at, :] = out.astype(BF16)
        log_sum[at, :] = jnp.where(lane_index(count) < HEAD, logs[1], logs[0])


def middle_kernel(
    cube, place, heads, tokens, cotangent, modul, proj_bias, h0, h1, h2, h3, h4, h5, h6, h7,
    branch, middle, mixed, gated_sum, weight, sem,
):
    rows, width = tokens.shape
    local = width // cube.tensor_size
    copies = start_pieces(cube, place, (h0, h1, h2, h3, h4, h5, h6, h7), (3 * local, local), weight, sem)
    for copy in copies:
        copy.wait()
    gain = 1.0 + modul[3:4, :]
    shift = modul[5:6, :]
    gamma = modul[0:1, :]
    gamma_two = modul[1:2, :]
    total = jnp.zeros((1, width), F32)
    for first, count in row_chunks(rows, 176):
        at = slice(first, first + count)
        out = proj_bias[0:1, :] + jnp.zeros((count, width), F32)
        for item in range(cube.tensor_size):
            out = out + dot_nt(
                heads[at, item * local : (item + 1) * local], weight[item]
            )
        branch[at, :] = out
        mid = tokens[at, :].astype(F32) + gamma * out
        middle[at, :] = mid
        centred, scale = moments(mid)
        mixed[0, at, :] = (centred * scale * gain + shift).astype(BF16)
        gated = (cotangent[at, :].astype(F32) * gamma_two).astype(BF16)
        mixed[1, at, :] = gated
        total += jnp.sum(gated.astype(F32), axis=0, keepdims=True)
    gated_sum[...] = total


def hidden_kernel(mixed, bias, matrix, hidden, slope):
    rows = mixed.shape[0]
    weight = matrix[...].reshape(mixed.shape[1], matrix.shape[2])
    for first, count in row_chunks(rows, 352):
        at = slice(first, first + count)
        pre = dot(mixed[at, :], weight) + bias[...]
        square = pre * pre
        bent = jnp.tanh(pre * (GELU_C + (GELU_C * GELU_A) * square))
        half = 0.5 * pre
        hidden[at, :] = (half + half * bent).astype(BF16)
        slope[at, :] = (
            0.5
            + 0.5 * bent
            + half * (1.0 - bent * bent) * (GELU_C + (3.0 * GELU_C * GELU_A) * square)
        )


def pre_back_kernel(slope, gated, matrix, grad_pre, bias_sums):
    weight = matrix[...].reshape(gated.shape[1], matrix.shape[2])
    low = (dot(gated[...], weight) * slope[...]).astype(BF16)
    grad_pre[...] = low
    bias_sums[...] = jnp.sum(low.astype(F32), axis=0, keepdims=True)


def add_products(total, left, matrix):
    weight = matrix[...].reshape(total.shape[1], matrix.shape[2])

    @pl.when(pl.program_id(0) == 0)
    def _():
        total[...] = dot_nt(left[...], weight)

    @pl.when(pl.program_id(0) > 0)
    def _():
        total[...] += dot_nt(left[...], weight)


def output_kernel(
    steps, hidden, matrix, cotangent, middle, modul, fc2_bias, output, sums,
    total, cotangent_here, middle_here, sem,
):
    step = pl.program_id(0)
    copies = [
        pltpu.make_async_copy(cotangent, cotangent_here, sem.at[0]),
        pltpu.make_async_copy(middle, middle_here, sem.at[1]),
    ]

    @pl.when(step == 0)
    def _():
        for copy in copies:
            copy.start()

    add_products(total, hidden, matrix)

    @pl.when(step == steps - 1)
    def _():
        for copy in copies:
            copy.wait()
        rows, width = total.shape
        gamma = modul[1:2, :]
        gamma_sum = jnp.zeros((1, width), F32)
        for first, count in row_chunks(rows, 64):
            at = slice(first, first + count)
            out = total[at, :] + fc2_bias[...]
            output[at, :] = (middle_here[at, :] + gamma * out).astype(BF16)
            gamma_sum += jnp.sum(
                cotangent_here[at, :].astype(F32) * out, axis=0, keepdims=True
            )
        sums[...] = gamma_sum


def first_back_kernel(
    cube, steps, place, grad_pre, matrix, middle, branch, cotangent, modul, h0, h1, h2, h3, h4, h5, h6, h7,
    g_middle, gated, g_heads, sums,
    total, middle_here, branch_here, cotangent_here, gated_here, small, sem, small_sem,
):
    step = pl.program_id(0)
    rows, width = total.shape
    narrow = small.shape[2]
    copies = [
        pltpu.make_async_copy(middle, middle_here, sem.at[0]),
        pltpu.make_async_copy(branch, branch_here, sem.at[1]),
        pltpu.make_async_copy(cotangent, cotangent_here, sem.at[2]),
    ]
    small_copies = make_pieces(
        cube, place, (h0, h1, h2, h3, h4, h5, h6, h7), (3 * narrow, narrow), small, small_sem
    )
    outs = [
        pltpu.make_async_copy(total, g_middle, sem.at[0]),
        pltpu.make_async_copy(gated_here, gated, sem.at[1]),
    ]

    @pl.when(step == 0)
    def _():
        for copy in copies + small_copies:
            copy.start()

    add_products(total, grad_pre, matrix)

    @pl.when(step == steps - 1)
    def _():
        for copy in copies:
            copy.wait()
        gain = 1.0 + modul[3:4, :]
        gamma = modul[0:1, :]
        totals = [jnp.zeros((1, width), F32) for _ in range(4)]
        for first, count in row_chunks(rows, 64):
            at = slice(first, first + count)
            grad = total[at, :]
            centred, scale = moments(middle_here[at, :])
            normed = centred * scale
            totals[0] += jnp.sum(grad * normed, axis=0, keepdims=True)
            totals[1] += jnp.sum(grad, axis=0, keepdims=True)
            lifted = grad * gain
            back = cotangent_here[at, :].astype(F32) + scale * (
                lifted
                - jnp.mean(lifted, axis=-1, keepdims=True)
                - normed * jnp.mean(lifted * normed, axis=-1, keepdims=True)
            )
            total[at, :] = back
            totals[2] += jnp.sum(back * branch_here[at, :], axis=0, keepdims=True)
            low = (back * gamma).astype(BF16)
            gated_here[at, :] = low
            totals[3] += jnp.sum(low.astype(F32), axis=0, keepdims=True)
        for place_at in range(4):
            sums[place_at : place_at + 1, :] = totals[place_at]
        for copy in outs:
            copy.start()
        for copy in small_copies:
            copy.wait()
        for item in range(cube.tensor_size):
            g_heads[:, item * narrow : (item + 1) * narrow] = dot(
                gated_here[...], small[item]
            ).astype(BF16)
        for copy in outs:
            copy.wait()


def core_rows(cube, place, target, source):
    rows, width = source.shape
    piece = width // cube.dp_size
    here = place[0] % 2 == 0
    for slab in range(width // LANES):
        flipped = source[:, slab * LANES : (slab + 1) * LANES].T
        for pair in range(LANES // (2 * piece)):
            at = 2 * pair * piece
            at_target = slab * LANES // 2 + pair * piece
            target[at_target : at_target + piece, :] = jnp.where(
                here, flipped[at : at + piece], flipped[at + piece : at + 2 * piece]
            )


def piece_copies(cube, place, relative, table, outs, sem, first, count):
    dp_at = place[0]
    item = jnp.bitwise_xor(place[1], relative)
    piece = table.shape[1] * 2 // cube.dp_size
    copies = []
    for part, order in enumerate(cube.sum_orders):
        half, rows = outs[2 * part].shape[0], outs[2 * part].shape[1]
        for index in range(2 * half):
            dp_mask, tensor_mask = cube.masks(order, index)
            if tensor_mask != relative:
                continue
            pair = jnp.bitwise_xor(dp_at, dp_mask) // 2
            row = pl.multiple_of(pair * piece + part * rows, 16)
            out = outs[2 * part + index // half]
            copies.append(
                pltpu.make_async_copy(
                    table.at[item, pl.ds(row, rows), :],
                    out.at[index % half, :, pl.ds(first, count)],
                    sem,
                )
            )
    return copies


def wide_grad_kernel(cube, per, place, left, left_far, right, right_far, *refs):
    outs, (flip, table, sem) = refs[:-3], refs[-3:]
    step = pl.program_id(0)
    local, block = table.shape[2], right.shape[1]

    @pl.when(step == 0)
    def _():
        core_rows(cube, place, flip.at[0], left)
        core_rows(cube, place, flip.at[1], left_far)

    got = (dot(flip[0], right[...]) + dot(flip[1], right_far[...])).astype(BF16)
    item = jnp.bitwise_xor(place[1], step // per)
    table[item, :, pl.ds(pl.multiple_of((step % per) * block, LANES), block)] = got
    for relative in range(cube.tensor_size):
        copies = piece_copies(cube, place, relative, table, outs, sem, 0, local)

        @pl.when(step == relative * per + per - 1)
        def _():
            for copy in copies:
                copy.start()

        @pl.when(step == cube.tensor_size * per - 1)
        def _():
            for copy in copies:
                copy.wait()


def qkv_grad_kernel(cube, with_proj, place, mixed, mixed_far, grads, grads_far, *refs):
    if with_proj:
        gated, gated_far, heads, heads_far = refs[:4]
        outs, refs = refs[4:8], refs[8:]
        flip, table, mat, mat_far, own, far, sem, in_sem, small, sides, sides_far = refs
    else:
        outs, refs = refs[:4], refs[4:]
        flip, table, mat, mat_far, own, far, sem, in_sem = refs
    copies = [
        pltpu.make_async_copy(source, target, in_sem.at[place_at])
        for place_at, (source, target) in enumerate(
            ((mixed, mat), (mixed_far, mat_far), (grads, own), (grads_far, far))
        )
    ]
    if with_proj:
        copies += [
            pltpu.make_async_copy(source, target, in_sem.at[4 + place_at])
            for place_at, (source, target) in enumerate(((heads, sides), (heads_far, sides_far)))
        ]
    for copy in copies:
        copy.start()
    local = table.shape[2] // 3
    for copy in copies[:2]:
        copy.wait()
    core_rows(cube, place, flip.at[0], mat)
    core_rows(cube, place, flip.at[1], mat_far)
    if with_proj:
        late = [
            pltpu.make_async_copy(source, target, in_sem.at[place_at])
            for place_at, (source, target) in enumerate(((gated, mat), (gated_far, mat_far)))
        ]
        for copy in late:
            copy.start()
    for copy in copies[2:4]:
        copy.wait()
    started = []
    for relative in range(cube.tensor_size):
        item = jnp.bitwise_xor(place[1], relative)
        cols = pl.ds(pl.multiple_of(item * local, LANES), local)
        for kind in range(3):
            table[item, :, kind * local : (kind + 1) * local] = (
                dot(flip[0], own[kind, :, cols]) + dot(flip[1], far[kind, :, cols])
            ).astype(BF16)
        group = piece_copies(cube, place, relative, table, outs, sem, 0, 3 * local)
        for copy in group:
            copy.start()
        started += group
    if with_proj:
        narrow = small.shape[2]
        for copy in late + copies[4:]:
            copy.wait()
        core_rows(cube, place, flip.at[0], mat)
        core_rows(cube, place, flip.at[1], mat_far)
        for relative in range(cube.tensor_size):
            item = jnp.bitwise_xor(place[1], relative)
            cols = pl.ds(pl.multiple_of(item * narrow, LANES), narrow)
            small[item] = (dot(flip[0], sides[:, cols]) + dot(flip[1], sides_far[:, cols])).astype(
                BF16
            )
            group = piece_copies(cube, place, relative, small, outs, sem, 3 * local, narrow)
            for copy in group:
                copy.start()
            started += group
    for copy in started:
        copy.wait()


def split_into(base, lanes, start, values):
    high = values.astype(BF16)
    rest = (values - high.astype(F32)).astype(BF16)
    base = jnp.where(lanes == start, high, base)
    return jnp.where(lanes == start + 1, rest, base)


def attend_back_kernel(
    query, key, value, grad, log_sum, r_query, r_key, head_scale, query_code, key_code,
    grads, sums, flat_query, sides, pairs,
):
    rows = query.shape[0]
    step = pairs.shape[1] // 2
    lanes = lane_index(rows)
    low = lanes < HEAD
    inner = lanes % HEAD
    q, k, v, g = query[...], key[...], value[...], grad[...]
    ones = head_ones(2 * LANES)
    spare = 16
    zero = jnp.zeros((rows, LANES), BF16)
    one = jnp.ones((rows, LANES), BF16)
    marks = (inner == spare) | (inner == spare + 1)

    @pl.when(pl.program_id(0) == 0)
    def _():
        pairs[...] = jnp.zeros_like(pairs)
        sides[...] = jnp.zeros_like(sides)

    qc = split_into(query_code[...], inner, spare, -log_sum[...])
    high = jnp.logical_not(low)
    q_wide = jnp.concatenate([q, qc], axis=1)
    for head in range(2):
        side = low if head == 0 else high
        k_code = jnp.where(marks & (high if head == 0 else low), one, key_code[...])
        k_side = jnp.where(side, k, zero)
        k_wide = jnp.concatenate([k_side, k_code], axis=1)
        v_side = jnp.where(side, v, zero)
        at = slice(head * step, head * step + rows)
        sides[0, at, :] = jnp.where(side, g, zero)
        sides[1, at, :] = jnp.where(side, q, zero)
        probs = jnp.exp(dot_nt(k_wide, q_wide))
        pairs[0:rows, at] = probs.astype(BF16)
        weighted = probs * dot_nt(v_side, g)
        change = (weighted - probs * jnp.sum(weighted, axis=0, keepdims=True)).astype(BF16)
        pairs[step : step + rows, at] = change
        flat = dot(k_side.T, change)
        if head == 0:
            flat_query[...] = flat
        else:
            flat_query[...] += flat
    d_value = dot(pairs[0:rows, :], sides[0]).astype(BF16)
    d_key = dot(pairs[step : step + rows, :], sides[1])
    d_query = flat_query[...].T
    scale = head_scale[0:1, :]
    unit = q.astype(F32) * (1.0 / scale)
    unit_key = k.astype(F32)
    both = head_sums(jnp.concatenate([unit * d_query, unit_key * d_key], axis=1), ones)
    along, along_key = both[:, :LANES], both[:, LANES:]
    out = (r_query[...] * scale * (d_query - unit * along)).astype(BF16)
    grads[0] = out
    sums[0:1, :] = jnp.sum(out.astype(F32), axis=0, keepdims=True)
    sums[2:3, :] = jnp.sum(along, axis=0, keepdims=True)
    grads[1] = (r_key[...] * (d_key - unit_key * along_key)).astype(BF16)
    grads[2] = d_value
    sums[1:2, :] = jnp.sum(d_value.astype(F32), axis=0, keepdims=True)


def last_kernel(cube, splits, place, modul, tokens, g_middle, *refs):
    held, refs = refs[:8], refs[8:]
    grads, refs = refs[: len(splits)], refs[len(splits) :]
    grad_tokens, sums, weight, left, tokens_here, middle_here, sem, in_sem = refs[:8]
    grads_here = refs[8:]
    rows, width = tokens_here.shape
    local = width // cube.tensor_size
    copies = [
        pltpu.make_async_copy(source, target, in_sem.at[place_at])
        for place_at, (source, target) in enumerate(
            list(zip(grads, grads_here)) + [(tokens, tokens_here), (g_middle, middle_here)]
        )
    ]
    for copy in copies:
        copy.start()
    pieces = make_pieces(cube, place, held, (0, weight.shape[2]), weight, sem)
    for copy in pieces:
        copy.start()
    for which, (start, size) in enumerate(splits):
        copies[which].wait()
        for item in range(cube.tensor_size):
            for kind in range(3):
                at = kind * local + start
                left[item, :, at : at + size] = grads_here[which][
                    kind, :, item * size : (item + 1) * size
                ]
    for copy in copies[len(splits) :] + pieces:
        copy.wait()
    gain = 1.0 + modul[2:3, :]
    totals = [jnp.zeros((1, width), F32) for _ in range(2)]
    for first, count in row_chunks(rows, 352):
        out = dot_nt(left[0, first : first + count, :], weight[0])
        for item in range(1, cube.tensor_size):
            out = out + dot_nt(left[item, first : first + count, :], weight[item])
        for inner, inner_count in row_chunks(count, 64):
            at = slice(first + inner, first + inner + inner_count)
            grad = out[inner : inner + inner_count]
            centred, scale = moments(tokens_here[at, :].astype(F32))
            normed = centred * scale
            totals[0] += jnp.sum(grad * normed, axis=0, keepdims=True)
            totals[1] += jnp.sum(grad, axis=0, keepdims=True)
            lifted = grad * gain
            back = middle_here[at, :] + scale * (
                lifted
                - jnp.mean(lifted, axis=-1, keepdims=True)
                - normed * jnp.mean(lifted * normed, axis=-1, keepdims=True)
            )
            grad_tokens[at, :] = back.astype(BF16)
    for place_at in range(2):
        sums[place_at : place_at + 1, :] = totals[place_at]


def pack_kernel(splits, sums_one, gamma_sum, sums_zero, fc1_bias_sum, gated_sum, *refs):
    parts, (out, side) = refs[: len(splits)], refs[len(splits) :]
    dp_size = side.shape[0]
    tensor_size = out.shape[0] // dp_size
    width = gamma_sum.shape[1]
    local, wide = width // tensor_size, fc1_bias_sum.shape[1] // tensor_size
    owners = LANES * dp_size // width
    for slab in range(width // LANES):
        cols = slice(slab * LANES, (slab + 1) * LANES)
        rows = slice(slab * owners, (slab + 1) * owners)
        side[rows, 0:LANES] = jnp.broadcast_to(gated_sum[:, cols], (owners, LANES))
        side[rows, LANES : 2 * LANES] = jnp.broadcast_to(sums_one[3:4, cols], (owners, LANES))
    modul = (
        sums_one[2:3, :], gamma_sum[...], sums_zero[0:1, :],
        sums_one[0:1, :], sums_zero[1:2, :], sums_one[1:2, :],
    )
    for item in range(tensor_size):
        rows = slice(item * dp_size, (item + 1) * dp_size)

        def put(at, values):
            count = values.shape[1]
            out[rows, at : at + count] = jnp.broadcast_to(values, (dp_size, count)).astype(BF16)

        for kind, values in enumerate(modul):
            put(kind * local, values[:, item * local : (item + 1) * local])
        for kind in range(3):
            for part, (start, size) in zip(parts, splits):
                at = (6 + kind) * local + start
                values = part[kind : kind + 1, item * size : (item + 1) * size]
                put(at, values)
                if kind == 2:
                    put(at + local, values - values.astype(BF16).astype(F32))
        put(10 * local, fc1_bias_sum[:, item * wide : (item + 1) * wide])
        out[rows, 10 * local + wide :] = side[...].astype(BF16)


def add_kernel(parts, groups, merge, *refs):
    outs = refs[4 * parts * groups :]
    at = 0
    for part in range(parts):
        first = 0
        for group in range(groups):
            for side in range(2):
                kept, received = refs[at], refs[at + 1]
                at += 2
                rows, count = kept.shape[1:]
                total = (kept[...].astype(F32) + received[...].astype(F32)).astype(BF16)
                base = part * rows if merge else 0
                out = outs[side] if merge else outs[2 * part + side]
                out[:, base : base + rows, first : first + count] = total
            first += count


def add_pieces(kept, received, merge):
    groups, parts = len(kept), len(kept[0])
    items, rows = kept[0][0].shape[0], kept[0][0].shape[1]
    half = items // 2
    per = max(1, half // 2)
    columns = sum(group[0].shape[2] for group in kept)
    operands, specs = [], []
    for part in range(parts):
        for group in range(groups):
            block = (per, rows, kept[group][part].shape[2])
            for side in range(2):
                spec = pl.BlockSpec(block, lambda i, side=side: (i + side * (half // per), 0, 0))
                operands += [kept[group][part], received[group][part]]
                specs += [spec, spec]
    out_rows, out_parts = (parts * rows, 1) if merge else (rows, parts)
    return pl.pallas_call(
        functools.partial(add_kernel, parts, groups, merge),
        out_shape=[jax.ShapeDtypeStruct((half, out_rows, columns), BF16)] * (2 * out_parts),
        grid=(half // per,),
        in_specs=specs,
        out_specs=[pl.BlockSpec((per, out_rows, columns), lambda i: (i, 0, 0))] * (2 * out_parts),
        cost_estimate=pl.CostEstimate(flops=1 << 20, bytes_accessed=1 << 20, transcendentals=0),
        compiler_params=pltpu.CompilerParams(vmem_limit_bytes=VMEM_BYTES),
        name="add",
    )(*operands)


def scale_codes(lengths, rows):
    count = lengths.shape[0]
    bounds = jnp.cumsum(lengths)
    places = jnp.arange(rows, dtype=jnp.int32)
    scale_of = jnp.sum((places[:, None] >= bounds[None, :]).astype(jnp.int32), axis=1)
    lane = jnp.arange(HEAD, dtype=jnp.int32)
    query_code = (scale_of[:, None] == lane[None, :]).astype(BF16)
    blocked = (scale_of[:, None] > lane[None, :]) & (lane[None, :] < count)
    key_code = jnp.where(blocked, MASKED, 0.0).astype(BF16)
    return jnp.tile(query_code, (1, 2)), jnp.tile(key_code, (1, 2))


def to_all(values, axes=AXES):
    return lax.all_to_all(values, axes, split_axis=0, concat_axis=0, tiled=True)


def local(
    tokens, condition, scale_lens, qkv_weight, qv_bias, head_scale, proj_weight, proj_bias,
    fc1_weight, fc1_bias, fc2_weight, fc2_bias, ada_weight, ada_bias, cotangent,
):
    dp_size, tensor_size = lax.axis_size("dp"), lax.axis_size("tensor")
    devices = dp_size * tensor_size
    cube = Cube(dp_size, tensor_size)
    dp_at, tensor_at = lax.axis_index("dp"), lax.axis_index("tensor")
    place = jnp.stack([dp_at, tensor_at]).astype(jnp.int32)
    rows, width = tokens.shape
    piece_rows = qkv_weight.shape[0]
    narrow = qkv_weight.shape[2]
    wide = fc1_weight.shape[1]
    hidden_width = wide * tensor_size

    cond_float = condition.astype(F32)
    cond_low = jax.nn.silu(cond_float).astype(BF16)
    cond_parts = cond_low.reshape(tensor_size, dp_size, piece_rows).transpose(1, 0, 2)
    cond_own = lax.all_to_all(cond_parts, "dp", split_axis=0, concat_axis=0, tiled=True)
    cond_back = cond_own.reshape(dp_size, tensor_size, piece_rows).transpose(1, 0, 2)
    cond_back = cond_back.reshape(devices, piece_rows)
    cond_own = cond_own.reshape(devices, piece_rows)
    ada_flat = ada_weight.reshape(piece_rows, 6 * narrow)

    narrow_gather = Gather(
        cube,
        jnp.concatenate([qkv_weight.reshape(piece_rows, 3 * narrow), proj_weight.T], axis=1),
    )
    narrow_gather.advance(cond_own)
    wide_shard = jnp.concatenate([fc1_weight, fc2_weight.T], axis=1)
    wide_all = lax.all_gather(
        behind(wide_shard, narrow_gather.held), AXES, axis=0, tiled=True
    ).reshape(dp_size, tensor_size, piece_rows, 2 * wide)
    while narrow_gather.step < cube.hops - 2:
        narrow_gather.advance()

    modul_part = jnp.dot(cond_own, ada_flat, preferred_element_type=F32)
    bias_part = jnp.where(dp_at == 0, ada_bias.astype(F32).reshape(1, 6 * narrow), 0.0)
    dp_part = jnp.concatenate([proj_bias, fc2_bias]).astype(F32)
    tensor_part = jnp.concatenate(
        [qv_bias.astype(F32).reshape(-1), jnp.repeat(head_scale, HEAD), fc1_bias.astype(F32)]
    )
    share = -(-tensor_part.shape[0] // (dp_size * LANES)) * LANES
    pieces = tensor_part.shape[0] // share
    tensor_share = lax.dynamic_index_in_dim(
        tensor_part.reshape(pieces, share), jnp.minimum(dp_at, pieces - 1), 0, keepdims=False
    )
    rest = jnp.concatenate([dp_part, tensor_share])[None]
    parts = to_all(
        jnp.concatenate(
            [modul_part + bias_part, jnp.broadcast_to(rest, (devices, rest.shape[1]))], axis=1
        )
    ).reshape(dp_size, tensor_size, -1)
    held = narrow_gather.sides(parts)
    rest = parts[:, 0, 6 * narrow :]
    proj_bias_full = rest[:, :piece_rows].reshape(1, width)
    fc2_bias_full = rest[:, piece_rows : 2 * piece_rows].reshape(1, width)

    own_lens = lax.dynamic_index_in_dim(scale_lens, tensor_at, 0, keepdims=False)
    query_code, key_code = scale_codes(own_lens, rows)

    dma = pltpu.SemaphoreType.DMA

    def half_shape(*dims):
        return shape(*dims, dtype=BF16)

    mixed_one, query, key, value, r_query, r_key, modul, fc1_bias_full, head_scale_full = call(
        functools.partial(front_kernel, cube, pieces),
        [half_shape(rows, width)] * 4
        + [shape(rows, width)] * 2
        + [shape(8, width), shape(1, hidden_width), shape(1, width)],
        [SMEM, VMEM, VMEM] + [ANY] * 8,
        [VMEM] * 9,
        [
            pltpu.VMEM((tensor_size, width, 3 * narrow), BF16),
            dma,
            pltpu.VMEM((2, width), F32),
        ],
        16, "front",
    )(place, tokens, parts, *held)
    mixed_one_far = cube.hop(mixed_one, cube.core)

    slab = pl.BlockSpec((rows, LANES), lambda i: (0, i))
    whole = pl.BlockSpec((rows, LANES), lambda i: (0, 0))
    heads, log_sum = call(
        attend_kernel,
        [half_shape(rows, width), shape(rows, width)],
        [slab] * 3 + [whole] * 2,
        [slab] * 2,
        [],
        20, "attend", grid=(width // LANES,),
    )(query, key, value, query_code, key_code)
    heads_far = cube.hop(heads, cube.core)

    branch, middle, mixed_two, gated_sum = call(
        functools.partial(middle_kernel, cube),
        [shape(rows, width)] * 2 + [half_shape(2, rows, width), shape(1, width)],
        [SMEM] + [VMEM] * 5 + [ANY] * 8,
        [VMEM] * 4,
        [pltpu.VMEM((tensor_size, width, narrow), BF16), dma],
        10, "middle", after=[mixed_one_far],
    )(place, heads, tokens, cotangent, modul, proj_bias_full, *held)
    mixed_two_far = cube.hop(mixed_two, cube.core)

    block = min(1024, wide)
    per = wide // block
    wide_steps = tensor_size * per

    def wide_block(first):
        return pl.BlockSpec(
            (dp_size, None, piece_rows, block), lambda i: (0, i // per, 0, first * per + i % per)
        )

    side = pl.BlockSpec((rows, block), lambda i: (0, i))
    side_row = pl.BlockSpec((1, block), lambda i: (0, i))

    def mixed_part(which):
        return pl.BlockSpec((None, rows, width), lambda i: (which, 0, 0))

    hidden, slope = call(
        hidden_kernel,
        [half_shape(rows, hidden_width), shape(rows, hidden_width)],
        [mixed_part(0), side_row, wide_block(0)],
        [side] * 2,
        [],
        20, "hidden", grid=(wide_steps,), after=[heads_far],
    )(mixed_two, fc1_bias_full, wide_all)
    hidden_far = cube.hop(hidden, cube.core)

    grad_pre, fc1_bias_sum = call(
        pre_back_kernel,
        [half_shape(rows, hidden_width), shape(1, hidden_width)],
        [side, mixed_part(1), wide_block(1)],
        [side, side_row],
        [],
        300, "pre_back", grid=(wide_steps,), after=[mixed_two_far],
    )(slope, mixed_two, wide_all)
    grad_pre_far = cube.hop(grad_pre, cube.core)

    def piece_shapes(columns):
        return [half_shape(devices // 4, piece_rows // 2, columns)] * 4

    def pairs(outs):
        return list(zip(outs[0::2], outs[1::2]))

    flip_scratch = pltpu.VMEM((2, width // 2, rows), BF16)
    grad_scratch = [flip_scratch, pltpu.VMEM((tensor_size, width // 2, wide), BF16), dma]

    def mixed_far_part(which):
        return pl.BlockSpec((None, rows, width), lambda i, at: (which, 0, 0))

    side_relative = pl.BlockSpec(
        (rows, block), lambda i, at: (0, jnp.bitwise_xor(at[1], i // per) * per + i % per)
    )

    def wide_grad(which, right, right_far, name, after):
        return call(
            functools.partial(wide_grad_kernel, cube, per),
            piece_shapes(wide),
            [mixed_far_part(which)] * 2 + [side_relative] * 2,
            [ANY] * 4,
            grad_scratch,
            300, name, grid=(wide_steps,), after=after, scalars=1,
        )(place, mixed_two, mixed_two_far, right, right_far)

    outs = wide_grad(1, hidden, hidden_far, "fc2_grad", [grad_pre])
    fc2_sum = Scatter(cube, [pairs(outs)])
    outs = wide_grad(0, grad_pre, grad_pre_far, "fc1_grad", [outs[0]])
    fc1_sum = Scatter(cube, [pairs(outs)])

    full = pltpu.VMEM((rows, width), F32)
    full_half = pltpu.VMEM((rows, width), BF16)
    whole_row = pl.BlockSpec((1, width), lambda i: (0, 0))
    eight_rows = pl.BlockSpec((8, width), lambda i: (0, 0))
    whole_half = pl.BlockSpec((rows, width), lambda i: (0, 0))
    g_middle, gated_one, g_heads, sums_one = call(
        functools.partial(first_back_kernel, cube, wide_steps),
        [
            shape(rows, width),
            half_shape(rows, width),
            half_shape(rows, width),
            shape(8, width),
        ],
        [SMEM, side, wide_block(0)] + [ANY] * 3 + [eight_rows] + [ANY] * 8,
        [ANY, ANY, whole_half, eight_rows],
        [
            full, full, full, full_half, full_half,
            pltpu.VMEM((tensor_size, width, narrow), BF16),
            dma((3,)), dma,
        ],
        500, "first_back", grid=(wide_steps,), after=[outs[0]],
    )(place, grad_pre, wide_all, middle, branch, cotangent, modul, *held)
    gated_one_far = cube.hop(gated_one, cube.core)

    splits = [(0, narrow // 2), (narrow // 2, narrow // 2)]
    if narrow < 2 * LANES:
        splits = [(0, narrow)]
    steps = narrow // LANES
    padded = -(-rows // LANES) * LANES

    def attend_back(start, size, after):
        per, base = size // LANES, start // LANES

        def column(i):
            return (i // per) * steps + base + i % per

        picked = pl.BlockSpec((rows, LANES), lambda i: (0, column(i)))
        picked_row = pl.BlockSpec((1, LANES), lambda i: (0, column(i)))
        count = tensor_size * per
        return call(
            attend_back_kernel,
            [half_shape(3, rows, count * LANES), shape(8, count * LANES)],
            [picked] * 7 + [picked_row] + [whole] * 2,
            [
                pl.BlockSpec((3, rows, LANES), lambda i: (0, 0, i)),
                pl.BlockSpec((8, LANES), lambda i: (0, i)),
            ],
            [
                pltpu.VMEM((LANES, rows), F32),
                pltpu.VMEM((2, 2 * padded, LANES), BF16),
                pltpu.VMEM((2 * padded, 2 * padded), BF16),
            ],
            400, "attend_back", grid=(count,), after=after,
        )(query, key, value, g_heads, log_sum, r_query, r_key, head_scale_full,
          query_code, key_code)

    def qkv_grad(size, with_proj, grads, grads_far, after):
        extra = [gated_one, gated_one_far, heads, heads_far] if with_proj else []
        cut = pltpu.VMEM((3, rows, tensor_size * size), BF16)
        proj_scratch = [pltpu.VMEM((tensor_size, width // 2, narrow), BF16), full_half, full_half]
        return call(
            functools.partial(qkv_grad_kernel, cube, with_proj),
            piece_shapes(3 * size + (narrow if with_proj else 0)),
            [SMEM] + [ANY] * (4 + len(extra)),
            [ANY] * 4,
            [
                flip_scratch,
                pltpu.VMEM((tensor_size, width // 2, 3 * size), BF16),
                full_half, full_half, cut, cut,
                dma, dma((6,)),
            ] + (proj_scratch if with_proj else []),
            200, "qkv_grad", after=after,
        )(place, mixed_one, mixed_one_far, grads, grads_far, *extra)

    after = fc2_sum.advance(sums_one)
    qkv_grads, qkv_grads_far, all_sums = [], [], []
    for start, size in splits:
        grads, part_sums = attend_back(start, size, after)
        qkv_grads.append(grads)
        all_sums.append(part_sums)
        qkv_grads_far.append(cube.hop(grads, cube.core))
        after = [grads] + fc2_sum.advance(part_sums) + fc1_sum.advance(part_sums)
        if len(all_sums) == 1:
            after += [gated_one_far]
    qkv_sum = Scatter(cube, [])
    for which, (start, size) in enumerate(splits):
        outs = qkv_grad(size, which == 0, qkv_grads[which], qkv_grads_far[which], after)
        qkv_sum.add(pairs(outs))
        after = [outs[0]]
    fc2_received = fc2_sum.received
    after += fc1_sum.advance(outs[0])
    output, gamma_sum = call(
        functools.partial(output_kernel, wide_steps),
        [half_shape(rows, width), shape(1, width)],
        [side, wide_block(1)] + [ANY] * 2 + [eight_rows, whole_row],
        [whole_half, whole_row],
        [full, full_half, full, dma((2,))],
        400, "output", grid=(wide_steps,), after=after + [fc2_received[0][0]],
    )(hidden, wide_all, cotangent, middle, modul, fc2_bias_full)
    fc1_received = fc1_sum.received
    after = qkv_sum.advance(gamma_sum) + [fc1_received[0][0]]
    grad_tokens, sums_zero = call(
        functools.partial(last_kernel, cube, splits),
        [half_shape(rows, width), shape(8, width)],
        [SMEM, VMEM] + [ANY] * (10 + len(splits)),
        [VMEM] * 2,
        [
            pltpu.VMEM((tensor_size, width, 3 * narrow), BF16),
            pltpu.VMEM((tensor_size, rows, 3 * narrow), BF16),
            full_half, full, dma, dma((2 + len(splits),)),
        ]
        + [pltpu.VMEM((3, rows, tensor_size * size), BF16) for start, size in splits],
        400, "last", after=after,
    )(place, modul, tokens, g_middle, *held, *qkv_grads)

    near_out = qkv_sum.advance(sums_zero)

    late = call(
        functools.partial(pack_kernel, splits),
        half_shape(devices, 10 * narrow + wide + 2 * LANES),
        [VMEM] * (5 + len(splits)),
        VMEM,
        [pltpu.VMEM((dp_size, 2 * LANES), F32)],
        1, "pack",
    )(sums_one, gamma_sum, behind(sums_zero, near_out), fc1_bias_sum, gated_sum, *all_sums)
    far_out = qkv_sum.advance(late)
    late = behind(to_all(late, BACK_AXES), far_out)
    fc2_own = fc2_sum.finish(far_out)
    fc1_own = fc1_sum.finish(far_out)
    grad_modul_all = late[:, : 6 * narrow]
    late_sum = jnp.sum(late.astype(F32), axis=0)
    grad_ada_bias = late_sum[: 6 * narrow].reshape(6, narrow)
    grad_qv_bias = late_sum[6 * narrow : 8 * narrow].reshape(2, narrow)
    head_sum = late_sum[8 * narrow : 9 * narrow] + late_sum[9 * narrow : 10 * narrow]
    grad_head_scale = head_sum.reshape(-1, HEAD)[:, 0]
    rest = late_sum[10 * narrow :]
    grad_fc1_bias = rest[:wide]
    first_own = (dp_at % (LANES // piece_rows)) * piece_rows
    own_rows = lax.dynamic_slice_in_dim(rest[wide:].reshape(2, LANES), first_own, piece_rows, axis=1)
    grad_fc2_bias, grad_proj_bias = own_rows[0], own_rows[1]
    grad_ada = lax.dot_general(
        cond_back, grad_modul_all, (((0,), (0,)), ((), ())), preferred_element_type=F32
    ).reshape(piece_rows, 6, narrow)
    cond_part = dot_nt(grad_modul_all, ada_flat)
    cond_all = to_all(cond_part, BACK_AXES).reshape(tensor_size, dp_size, piece_rows)
    own = qkv_sum.finish(cond_part)
    parts_own, first = [], 0
    for which, (start, size) in enumerate(splits):
        parts_own.append(own[:, first : first + 3 * size].reshape(piece_rows, 3, size))
        first += 3 * size
        if which == 0:
            proj_own = own[:, first : first + narrow].T
            first += narrow
    qkv_own = jnp.concatenate(parts_own, axis=2)

    cond_image = lax.dynamic_slice_in_dim(cond_float, tensor_at, 1, axis=0)
    unused, silu_back = jax.vjp(jax.nn.silu, cond_image)
    grad_condition = silu_back(jnp.sum(cond_all, axis=0).reshape(1, width))[0]

    return (
        output,
        grad_tokens,
        grad_condition,
        qkv_own,
        grad_qv_bias,
        grad_head_scale,
        proj_own,
        grad_proj_bias,
        fc1_own,
        grad_fc1_bias,
        fc2_own.T,
        grad_fc2_bias,
        grad_ada,
        grad_ada_bias,
    )


def solution(mesh):
    return jax.shard_map(
        local,
        mesh=mesh,
        in_specs=(
            P(("dp", "tensor"), None),
            P("dp", None),
            P("dp", None),
            P("dp", None, "tensor"),
            P(None, "tensor"),
            P("tensor"),
            P("tensor", "dp"),
            P("dp"),
            P("dp", "tensor"),
            P("tensor"),
            P("tensor", "dp"),
            P("dp"),
            P("dp", None, "tensor"),
            P(None, "tensor"),
            P(("dp", "tensor"), None),
        ),
        out_specs=(
            P(("dp", "tensor"), None),
            P(("dp", "tensor"), None),
            P(("dp", "tensor"), None),
            P("dp", None, "tensor"),
            P(None, "tensor"),
            P("tensor"),
            P("tensor", "dp"),
            P("dp"),
            P("dp", "tensor"),
            P("tensor"),
            P("tensor", "dp"),
            P("dp"),
            P("dp", None, "tensor"),
            P(None, "tensor"),
        ),
        check_vma=False,
    )
```
